256 devices in a mesh: dp: 8 (over x, core), tm: 8 (over z), space: 4 (over y).
Axes of the slice: x: 4, y: 4, z: 8, core: 2. Of those that a mesh axis runs over, the one named last changes fastest.
Arguments:
- latents: bfloat16 [8, 16, 8, 128, 512], P('dp', 'tm', 'space'), may hold values from -400 to 400
- owner: int32 [8, 4, 1], P('dp'), may hold values from 0 to 3; in each aligned block of 4 rows (0 to 3, 4 to 7, ..., all dimensions but the last counted through in order) at most 2 rows name the same one
- gamma: float32 [512], replicated, may hold values from 0.25 to 1.75
- beta: float32 [512], replicated, may hold values from -3 to 3
- weight: bfloat16 [512, 27, 256], P(('dp', 'tm', 'space')), may hold values from -0.0546875 to 0.0546875
- upstream: bfloat16 [8, 16, 4, 512, 256], P('dp', 'tm', 'space'), may hold values from -20 to 20
Outputs:
- dlatents: bfloat16 [8, 16, 8, 128, 512], P('dp', 'tm', 'space')
- dweight: float32 [512, 27, 256], P(('dp', 'tm', 'space'))
- dgamma: float32 [512], replicated
- dbeta: float32 [512], replicated
The draws below stay inside these ranges and needn't reach their ends.
Inputs may be any that keep to these rules, and one draw needn't show every extreme that they name: `owner`: in every clip each of the 4 owners is named by at most 2 of the 4 tiles, and by exactly 2 in some clips.
All inputs are finite; a program needn't handle non-finite values.
Results may differ from the reference program's by a relative error of at most 0.002.
The reference program's roundings to bfloat16 on the way count: a program that leaves them out, or rounds other values in their place, can miss the bound.
Values may be sent and summed in bfloat16 or wider, within the bound.
A program may use at most 128 MiB of HBM per device.

```python
import math
import jax
import jax.numpy as jnp
import numpy as np
from jax import lax

C = 512
COUT = 256
GROUPS = 32
TH = 8
TW = 16
GSIZE = 16
CAP = 2
CLIPS = 8
FR = 16
TILES = 4
SLOTS = 8
N_SPACE = 4


def draw_latents(key, part):
    keys = jax.random.split(key, 4)
    shape = (CLIPS, FR, SLOTS, TH * TW, C)
    base = jax.random.normal(keys[0], shape, jnp.float32)
    offset = 0.5 * jax.random.normal(keys[1], (CLIPS, 1, 1, 1, C), jnp.float32)
    frame_scale = 1.0 + 2.0 * jnp.arange(FR, dtype=jnp.float32) / (FR - 1)
    chan_scale = jnp.exp(jax.random.uniform(keys[2], (C,), jnp.float32, -1.2, 1.2))
    slot_scale = jnp.exp(jax.random.uniform(keys[3], (CLIPS, FR, SLOTS, 1, 1), jnp.float32, 0.0, 1.1))
    values = base * frame_scale[None, :, None, None, None] * chan_scale * slot_scale + offset
    return values.astype(jnp.bfloat16)


def draw_upstream(key, part):
    keys = jax.random.split(jax.random.fold_in(key, 77), 2)
    shape = (CLIPS, FR, TILES, 4 * TH * TW, COUT)
    ramp = jnp.arange(FR, dtype=jnp.float32) / (FR - 1)
    base = jnp.clip(jax.random.normal(keys[0], shape, jnp.float32), -4.0, 4.0)
    offset = jnp.clip(0.6 * jax.random.normal(keys[1], (CLIPS, 1, 1, 1, COUT), jnp.float32), -2.0, 2.0)
    frame_scale = 0.4 + 2.0 * ramp
    values = (base + offset) * frame_scale[None, :, None, None, None]
    return values.astype(jnp.bfloat16)


def level_of(stream_key, extent, cuts, smallest, largest):
    def one(dim, parts):
        heights = jax.random.uniform(jax.random.fold_in(jax.random.fold_in(stream_key, 6), dim), (parts,), jnp.float32, smallest / len(cuts), largest / len(cuts))
        return jnp.repeat(jnp.exp(heights), extent[dim] // parts).reshape((-1,) + (1,) * (len(extent) - dim - 1))

    gain = one(*cuts[0])
    for cut in cuts[1:]:
        gain = gain * one(*cut)
    return gain


def shared_out(own_key, own, number, rows, count, top, reach, lean):
    sequence = jax.random.permutation(own_key, count)
    heavy_load, ordinary = load_shares(count, rows * top, reach, lean, True), load_shares(count, rows * top, reach, lean, False)
    places = jnp.arange(count)

    def named(tallies, turn):
        used = int((tallies > 0).sum())
        fixed = max(1, used // 4)
        moved = fixed + (places - fixed + turn * (used - fixed)) % max(1, count - fixed)
        return jnp.zeros((count,), jnp.int32).at[sequence[jnp.where(places < fixed, places, moved)]].set(jnp.asarray(tallies, jnp.int32))

    tallies = jnp.where(number % 4 == 0, named(heavy_load, number // 4), named(ordinary, number - number // 4 - 1))
    mixed = jax.random.permutation(jax.random.fold_in(own, 3), count)
    donor, taker = mixed[0:count // 2 * 2:2], mixed[1:count // 2 * 2:2]
    slack = jnp.minimum(tallies[donor] - 1, reach - tallies[taker]) // 2
    slack = jnp.where((donor == sequence[0]) | (taker == sequence[0]) | (tallies[taker] == 0), 0, jnp.maximum(slack, 0))
    moved = jax.random.randint(jax.random.fold_in(own, 4), (count // 2,), 0, 1 << 20) % (slack + 1)
    tallies = tallies.at[donor].add(-moved).at[taker].add(moved)
    items = jnp.searchsorted(jnp.cumsum(tallies), jnp.arange(rows * top), side="right").astype(jnp.int32)
    grid = items.reshape(top, rows).T
    grid = grid[jax.random.permutation(jax.random.fold_in(own, 1), rows)]
    turn = jax.random.randint(jax.random.fold_in(own, 2), (rows, 1), 0, top)
    return jnp.take_along_axis(grid, (jnp.arange(top)[None, :] + turn) % top, axis=1)


def load_shares(number_of, total, most, skew, full):
    loads = [(1 << 20) // math.isqrt(grade ** skew) + 1 for grade in range(1, number_of + 1)]
    largest = most if full else min(most, max(-(-total // number_of), total * loads[0] // sum(loads)))
    least = 1 if total - largest >= number_of - 1 else 0
    given, spare = [largest] + [least] * (number_of - 1), total - largest - least * (number_of - 1)
    while spare > 0:
        free = [i for i in range(1, number_of) if given[i] < largest] or [i for i in range(1, number_of) if given[i] < most]
        pool, budget = sum([loads[i] for i in free]), spare
        for i in free:
            more = min(most - given[i], max(1, budget * loads[i] // pool), spare)
            given[i] = given[i] + more
            spare = spare - more
    return np.array(given)


def normal_values(rng, dims, deviation, most, shards=(), kind=jnp.bfloat16):
    array = deviation * jax.random.normal(rng, dims, jnp.float32)
    if shards:
        array = array * level_of(rng, dims, shards, -0.22, 0.18)
    return jnp.clip(array, -most, most).astype(kind)


def setup_inputs(seed: int = 0) -> dict:
    seeds = jax.random.split(jax.random.key(seed), 7)
    latents = draw_latents(jax.random.fold_in(seeds[6], 71), 0)
    owner_keys = jax.random.split(jax.random.fold_in(seeds[1], 1), CLIPS * TILES // TILES)
    owner_turns = jax.random.permutation(jax.random.fold_in(seeds[1], 3), CLIPS * TILES // TILES)
    owner = jax.vmap(lambda own, number: shared_out(jax.random.fold_in(seeds[1], 2), own, number, TILES, N_SPACE, 1, CAP, 2))(owner_keys, owner_turns).reshape((CLIPS, TILES, 1))
    gamma = jnp.clip(1.0 + 0.15 * jax.random.normal(seeds[2], (C,), jnp.float32), 0.25, 1.75)
    beta = normal_values(seeds[3], (C,), 0.5, 3.0, (), jnp.float32)
    weight = normal_values(seeds[4], (C, 27, COUT), (27 * C) ** -0.5, 0.0546875, ((0, 256),))
    upstream = draw_upstream(jax.random.fold_in(seeds[6], 71), 0)
    return {"latents": latents, "owner": owner, "gamma": gamma, "beta": beta, "weight": weight, "upstream": upstream}


EPS = 1e-06

def tap_list():
    return [(kt, ky, kx) for kt in range(3) for ky in range(3) for kx in range(3)]

def clip_grads(latent, upper, owned, gamma, beta, weight):
    hot = (owned[:, None] == jnp.arange(N_SPACE, dtype=jnp.int32)[None, :]).astype(jnp.int32)
    rank = lax.optimization_barrier(jnp.sum((jnp.cumsum(hot, axis=0).astype(jnp.int32) - hot) * hot, axis=1)).astype(jnp.int32)
    slot = (owned * CAP + rank).astype(jnp.int32)
    cells = TH * TW
    values = latent[:, slot].astype(jnp.float32)
    grouped = values.reshape(FR, TILES, cells, GROUPS, GSIZE)
    mean = lax.optimization_barrier(jnp.mean(grouped, axis=(0, 1, 2, 4)))
    centred = grouped - mean[:, None]
    var = lax.optimization_barrier(jnp.mean(centred * centred, axis=(0, 1, 2, 4)))
    inverse = lax.rsqrt(var + EPS)
    normed = (centred * inverse[:, None]).reshape(FR, TILES, cells, C)
    act = normed * gamma + beta
    sig = jax.nn.sigmoid(act)
    hidden = (act * sig).astype(jnp.bfloat16)
    pooled = upper.astype(jnp.float32).reshape(FR, TILES, TH, 2, TW, 2, COUT)
    grads = lax.optimization_barrier(jnp.sum(pooled, axis=(3, 5))).reshape(FR, TILES, cells, COUT).astype(jnp.bfloat16)
    extended = jnp.concatenate([hidden[:1], hidden[:1], hidden], axis=0).reshape(FR + 2, TILES, TH, TW, C)
    padded = jnp.pad(extended, ((0, 0), (0, 0), (1, 1), (1, 1), (0, 0)))
    rows = grads.reshape(FR * TILES * cells, COUT)
    terms = []
    dext = jnp.zeros((FR + 2, TILES, TH + 2, TW + 2, C), jnp.float32)
    for index, (kt, ky, kx) in enumerate(tap_list()):
        tap = padded[kt:kt + FR, :, ky:ky + TH, kx:kx + TW].reshape(FR * TILES * cells, C)
        terms.append(lax.dot_general(tap, rows, (((0,), (0,)), ((), ())), preferred_element_type=jnp.float32))
        back = lax.dot_general(rows, weight[:, index, :], (((1,), (1,)), ((), ())), preferred_element_type=jnp.float32)
        dext = dext.at[kt:kt + FR, :, ky:ky + TH, kx:kx + TW].add(back.reshape(FR, TILES, TH, TW, C))
    dweight = jnp.stack(terms, axis=1)
    dinner = dext[:, :, 1:TH + 1, 1:TW + 1].reshape(FR + 2, TILES, cells, C)
    dhidden = dinner[2:]
    dhidden = dhidden.at[0].add(dinner[0] + dinner[1])
    dact = dhidden * (sig * (1.0 + act * (1.0 - sig)))
    dgain = lax.optimization_barrier(jnp.sum(dact * normed, axis=(0, 1, 2)))
    dshift = lax.optimization_barrier(jnp.sum(dact, axis=(0, 1, 2)))
    dnorm = (dact * gamma).reshape(FR, TILES, cells, GROUPS, GSIZE)
    ngroup = normed.reshape(FR, TILES, cells, GROUPS, GSIZE)
    first_m = lax.optimization_barrier(jnp.mean(dnorm, axis=(0, 1, 2, 4)))
    second_m = lax.optimization_barrier(jnp.mean(dnorm * ngroup, axis=(0, 1, 2, 4)))
    dvalues = inverse[:, None] * (dnorm - first_m[:, None] - ngroup * second_m[:, None])
    dfull = dvalues.reshape(FR, TILES, cells, C)
    dfull = dfull.at[..., :COUT].add(grads.astype(jnp.float32))
    dslots = jnp.zeros((FR, SLOTS, cells, C), jnp.bfloat16).at[:, slot].set(dfull.astype(jnp.bfloat16))
    return (dslots, dweight, dgain, dshift)

def reference(latents, owner, gamma, beta, weight, upstream):

    def step(carry, item):
        latent, upper, owned = item
        dslots, dweight, dgain, dshift = clip_grads(latent, upper, owned, gamma, beta, weight)
        return ((carry[0] + dweight, carry[1] + dgain, carry[2] + dshift), dslots)
    start = (jnp.zeros((C, 27, COUT), jnp.float32), jnp.zeros((C,), jnp.float32), jnp.zeros((C,), jnp.float32))
    sums, dlatents = lax.scan(step, start, (latents, upstream, owner[:, :, 0]))
    rscale = 1.0 / math.sqrt(CLIPS * FR * TILES * TH * TW)
    return (dlatents, sums[0] * rscale, sums[1] * rscale, sums[2] * rscale)
```

```python
import math

import jax
import jax.numpy as jnp
from jax import lax
from jax.experimental import pallas as pl
from jax.experimental.pallas import tpu as pltpu
from jax.sharding import PartitionSpec as P

MESH = pl.DeviceIdType.MESH
F32 = jnp.float32
BF16 = jnp.bfloat16
EPS = 1e-06

NDP, NTM, NSP = 8, 8, 4
GROUPS = 32
GS = 16
FR = 16
TILES = 4
CAP = 2
TH, TW = 8, 16
CELLS = TH * TW
C, COUT = 512, 256
TAPS = 27
ROWS = 9 * GS
LEFT = 48

B_TM, B_SP, A_SP, A_TM = 0, 8, 40, 44
L_SP, L_TM, WGT = 52, 56, 64
D_TM, D_DP, G_DP, D_SP, D_OWN, G_ALL = 72, 80, 88, 96, 100, 101
N_SEM = 133


def body(
    owner_ref, gamma_ref, beta_ref, lat_ref, ups_ref, w_ref,
    dlat_ref, dw_ref, dgb_ref,
    gz, ybuf, zsend, xbuf, wbuf, wf, wk, a9, xh, ds, dhb, rsd, dk, dsend, drecv, dsum,
    dxs, zback, tback, ysend, gown, gdp, gsum, gall, send_sem, recv_sem, own_sem,
):
    d, z, y = lax.axis_index("dp"), lax.axis_index("tm"), lax.axis_index("space")
    ahead = lambda v, r, n: lax.rem(v + r, n)
    behind = lambda v, r, n: lax.rem(v - r + n, n)
    line = (d * NTM + z) * NSP + y
    mine = y * NTM + z
    w_group = line // 8
    w_tm, w_sp = lax.rem(w_group, NTM), w_group // NTM
    w_piece = lax.rem(line, 8)
    src = lambda i: {
        "dp": mine // 4,
        "tm": 2 * lax.rem(mine, 4) + i // 4,
        "space": lax.rem(jnp.int32(i), 4) if not isinstance(i, int) else i % 4,
    }
    w_self = (w_tm == z) & (w_sp == y)
    own_piece_here = line // 8 == mine

    started = []

    def copy(a, b, n, to, m=None):
        return pltpu.make_async_remote_copy(
            src_ref=a, dst_ref=b, send_sem=send_sem.at[n], recv_sem=recv_sem.at[n if m is None else m],
            device_id=to, device_id_type=MESH,
        )

    def go(a, b, n, to, m=None):
        c = copy(a, b, n, to, m)
        c.start()
        started.append(c)
        return c

    def got(region, n):
        copy(region, region, n, {"tm": z}).wait_recv()

    barrier = pltpu.get_barrier_semaphore()

    def greet(to):
        pl.semaphore_signal(barrier, inc=1, device_id=to, device_id_type=MESH)

    for r in range(NTM):
        for q in range(NSP):
            if r or q:
                greet({"tm": ahead(z, r, NTM), "space": ahead(y, q, NSP)})
    for r in range(1, NDP):
        greet({"dp": ahead(d, r, NDP)})
    for i in range(8):
        o = src(i)

        @pl.when((8 * mine + i) != line)
        def _():
            greet(o)

    @pl.when(jnp.logical_not(own_piece_here & (w_piece == d)))
    def _():
        greet({"dp": w_piece, "tm": w_tm, "space": w_sp})

    p = lax.broadcasted_iota(jnp.int32, (CELLS, 4 * CELLS), 0)
    q = lax.broadcasted_iota(jnp.int32, (CELLS, 4 * CELLS), 1)
    pool = ((q >> 6) == (p >> 4)) & (((q & 31) >> 1) == (p & 15))
    pool = jnp.where(pool, 1.0, 0.0).astype(BF16)
    for f in range(2):
        pooled = jnp.dot(pool, ups_ref[f], preferred_element_type=F32)
        gz[2 + 2 * z + f, y] = pooled.astype(BF16)
    for f in (0, 1, FR + 2, FR + 3):
        gz[f] = jnp.zeros((TILES, CELLS, COUT), BF16)

    self_w = jnp.where(w_self, 1, 0)
    self_o = jnp.where(own_piece_here & (w_piece == d), 1, 0)
    self_s = jnp.where(own_piece_here, 1, 0)
    own_to = 8 * mine + d
    self_t = jnp.where(own_to == line, 1, 0)
    pl.semaphore_wait(barrier, NTM * NSP - 1 + NDP - 1 + 8 - self_s + 1 - self_t)

    def part_b(zo, yo, f=0, n=2):
        return gz.at[pl.ds(2 + 2 * zo + f, n), yo, pl.ds(LEFT, CELLS - LEFT)]

    def part_a(zo, yo, f=0, n=2):
        return gz.at[pl.ds(2 + 2 * zo + f, n), yo, pl.ds(0, LEFT)]

    def row_a(zo, f=0, n=2):
        return gz.at[pl.ds(2 + 2 * zo + f, n), :, pl.ds(0, LEFT)]

    zr, zl = {"tm": ahead(z, 1, NTM)}, {"tm": behind(z, 1, NTM)}
    yr, yl = {"space": ahead(y, 1, NSP)}, {"space": behind(y, 1, NSP)}
    yo_r, yo_l, yo_2 = ahead(y, 1, NSP), behind(y, 1, NSP), ahead(y, 2, NSP)

    def tm_step(region, base, h):
        frames = (dict(f=0, n=2),) * 2 if h < 4 else (dict(f=0, n=1), dict(f=1, n=1))
        for way, (to, o) in enumerate(((zr, behind(z, h - 1, NTM)), (zl, ahead(z, h - 1, NTM)))):
            a = region(o, **frames[way])
            go(a, a, base + 2 * (h - 1) + way, to)

    def tm_got(region, base, h):
        frames = (dict(f=0, n=2),) * 2 if h < 4 else (dict(f=0, n=1), dict(f=1, n=1))
        for way, o in enumerate((behind(z, h, NTM), ahead(z, h, NTM))):
            got(region(o, **frames[way]), base + 2 * (h - 1) + way)

    def sp_send(region, base, zo):
        a = region(zo, y)
        go(a, a, base, yr)
        go(a, a, base + 1, yl)

    def sp_forward(region, base, zo):
        got(region(zo, yo_l), base)
        a = region(zo, yo_l, 0, 1)
        go(a, a, base + 2, yr)
        got(region(zo, yo_r), base + 1)
        a = region(zo, yo_r, 1, 1)
        go(a, a, base + 3, yl)

    def sp_got(region, base, zo):
        got(region(zo, yo_2, 0, 1), base + 2)
        got(region(zo, yo_2, 1, 1), base + 3)

    steps = (0, -1, 1, -2, 2, -3, 3, 4)
    origin = [lax.rem(z + s + NTM, NTM) for s in steps]
    b_row = lambda zo, yo, f=0, n=2: part_b(zo, yo, f, n)
    b_tm = lambda zo, f=0, n=2: part_b(zo, y, f, n)

    for r in range(1, NSP):
        yo = ahead(y, r, NSP)
        go(
            lat_ref.at[:, :, :, pl.ds(pl.multiple_of(yo * 128, 128), 128)],
            ybuf.at[y], L_SP + r, {"space": yo},
        )
    own = pltpu.make_async_copy(
        lat_ref.at[:, :, :, pl.ds(pl.multiple_of(y * 128, 128), 128)], ybuf.at[y], own_sem.at[0]
    )
    own.start()
    tm_step(b_tm, B_TM, 1)
    sp_send(part_a, A_SP, z)
    sp_send(b_row, B_SP, origin[0])

    for r in range(NDP):
        to = {"dp": ahead(d, r, NDP), "tm": w_tm, "space": w_sp}
        c = copy(w_ref, wbuf.at[w_piece], WGT + r, to, WGT + w_piece)
        if r:
            c.start()
            started.append(c)
        else:

            @pl.when(jnp.logical_not(w_self))
            def _():
                c.start()

            @pl.when(w_self)
            def _():
                pltpu.make_async_copy(w_ref, wbuf.at[w_piece], recv_sem.at[WGT + w_piece]).start()

    sp_forward(part_a, A_SP, z)
    tm_got(b_tm, B_TM, 1)
    tm_step(b_tm, B_TM, 2)
    sp_send(b_row, B_SP + 4, origin[1])
    sp_send(b_row, B_SP + 8, origin[2])

    own.wait()
    for r in range(1, NSP):
        got(ybuf.at[behind(y, r, NSP)], L_SP + r)
    owners = [owner_ref[0, t, 0] for t in range(TILES)]
    ranks = [
        jnp.minimum(
            sum([(owners[u] == owners[t]).astype(jnp.int32) for u in range(t)], jnp.int32(0)), CAP - 1
        )
        for t in range(TILES)
    ]
    for t in range(TILES):
        for f in range(2):
            v = ybuf[owners[t], f, ranks[t]].astype(F32)
            zsend[:, f * TILES + t] = v.T.reshape(NTM, GS, CELLS).astype(BF16)
    for r in range(1, NTM):
        zo = ahead(z, r, NTM)
        go(zsend.at[zo], xbuf.at[z], L_TM + r, {"tm": zo})
    xbuf[z] = zsend[z]

    sp_got(part_a, A_SP, z)
    tm_step(row_a, A_TM, 1)
    sp_forward(b_row, B_SP, origin[0])
    tm_got(b_tm, B_TM, 2)
    tm_step(b_tm, B_TM, 3)
    sp_send(b_row, B_SP + 12, origin[3])
    sp_send(b_row, B_SP + 16, origin[4])
    sp_forward(b_row, B_SP + 4, origin[1])
    sp_forward(b_row, B_SP + 8, origin[2])
    tm_got(b_tm, B_TM, 3)
    tm_step(b_tm, B_TM, 4)
    sp_send(b_row, B_SP + 20, origin[5])
    sp_send(b_row, B_SP + 24, origin[6])
    tm_got(row_a, A_TM, 1)
    tm_step(row_a, A_TM, 2)
    sp_forward(b_row, B_SP + 12, origin[3])
    sp_forward(b_row, B_SP + 16, origin[4])
    tm_got(b_tm, B_TM, 4)
    sp_send(b_row, B_SP + 28, origin[7])
    tm_got(row_a, A_TM, 2)
    tm_step(row_a, A_TM, 3)
    sp_forward(b_row, B_SP + 20, origin[5])
    sp_forward(b_row, B_SP + 24, origin[6])
    tm_got(row_a, A_TM, 3)
    tm_step(row_a, A_TM, 4)
    sp_forward(b_row, B_SP + 28, origin[7])

    for r in range(1, NTM):
        got(xbuf.at[behind(z, r, NTM)], L_TM + r)
    count = float(FR * TILES * CELLS * GS)
    zero = jnp.zeros((GS, CELLS), F32)

    def whole(v):
        return jnp.sum(jnp.sum(v, axis=1, keepdims=True), axis=0, keepdims=True)

    def total(i, acc):
        return acc + jnp.sum(xbuf[i].astype(F32), axis=0)

    mean = whole(lax.fori_loop(0, NTM, total, zero)) / count

    def spread(i, acc):
        v = xbuf[i].astype(F32) - mean
        return acc + jnp.sum(v * v, axis=0)

    inverse = lax.rsqrt(whole(lax.fori_loop(0, NTM, spread, zero)) / count + EPS)

    row16 = lax.broadcasted_iota(jnp.int32, (GS, CELLS), 0)
    lane16 = lax.broadcasted_iota(jnp.int32, (GS, CELLS), 1)
    diag = lane16 == z * GS + row16

    def column(ref):
        return jnp.sum(jnp.where(diag, ref[pl.ds(y, 1), :], 0.0), axis=1, keepdims=True)

    gamma, beta = column(gamma_ref), column(beta_ref)

    cell = lax.broadcasted_iota(jnp.int32, (8, GS, CELLS), 2)
    ix, iy = cell & (TW - 1), cell >> 4

    def inside(dy, dx):
        ok = None
        for cond in (
            [iy + dy >= 0] if dy < 0 else [iy + dy < TH] if dy > 0 else []
        ) + ([ix + dx >= 0] if dx < 0 else [ix + dx < TW] if dx > 0 else []):
            ok = cond if ok is None else ok & cond
        return ok

    def taps(i, _):
        normed = (xbuf[i].astype(F32) - mean) * inverse
        act = normed * gamma + beta
        sig = jax.nn.sigmoid(act)
        xh[i] = normed
        ds[i] = sig * (1.0 + act * (1.0 - sig))
        hidden = (act * sig).astype(BF16).astype(F32)
        base = pl.multiple_of((i + 1) * 1024, 1024)
        for s in range(9):
            dy, dx = s // 3 - 1, s % 3 - 1
            v = hidden
            if s != 4:
                v = pltpu.roll(v, (-(TW * dy + dx)) % CELLS, 2)
                v = jnp.where(inside(dy, dx), v, 0.0)
            v = v.astype(BF16)
            for j in range(8):
                a9[s * GS : (s + 1) * GS, pl.ds(base + j * CELLS, CELLS)] = v[j]
        return 0

    lax.fori_loop(0, NTM, taps, 0)
    a9[:, 0:512] = a9[:, 1024:1536]
    a9[:, 512:1024] = a9[:, 1024:1536]

    for i in range(8):
        got(wbuf.at[i], WGT + i)
    for i in range(8):
        wf[:, 2 * i : 2 * i + 2, :] = wbuf[i].astype(F32)
    for kt in range(3):
        wk[kt, 0:ROWS, :] = wf[9 * kt : 9 * kt + 9].reshape(ROWS, COUT).astype(BF16)
    pick_r = lax.broadcasted_iota(jnp.int32, (GS, COUT), 0)
    pick_o = lax.broadcasted_iota(jnp.int32, (GS, COUT), 1)
    wk[0, ROWS : ROWS + GS, :] = jnp.where(pick_o == mine * GS + pick_r, 1.0, 0.0).astype(BF16)

    for i in range(8):
        sp_got(b_row, B_SP + 4 * i, origin[i])
    tm_got(row_a, A_TM, 4)

    dk[...] = jnp.zeros_like(dk)

    def dweight(i, _):
        g = gz[pl.ds(2 + 2 * i, 2)].reshape(1024, COUT)
        for kt in range(3):
            a = a9[:, pl.ds(pl.multiple_of(1024 * i + 512 * kt, 512), 1024)]
            dk[9 * kt : 9 * kt + 9] += jnp.dot(a, g, preferred_element_type=F32).reshape(9, GS, COUT)
        return 0

    lax.fori_loop(0, NTM, dweight, 0)
    rscale = 1.0 / math.sqrt(NDP * FR * TILES * CELLS)
    for i in range(8):
        dsend[i] = dk[:, 2 * i : 2 * i + 2, :] * rscale
    for r in range(1, NDP):
        to = ahead(d, r, NDP)
        go(dsend.at[to], drecv.at[d], D_DP + r, {"dp": to})
    drecv[d] = dsend[d]

    nt = (((1,), (1,)), ((), ()))

    def back(e, _):
        sums = None
        for kt in range(3):
            g = gz[e + 2 - kt].reshape(512, COUT)
            w = wk[kt] if kt == 0 else wk[kt, 0:ROWS, :]
            v = lax.dot_general(w, g, nt, preferred_element_type=F32)
            if kt == 0:
                rest, sums = v[ROWS:], v[:ROWS]
            else:
                sums = sums + v
        for t in range(TILES):
            out = None
            for s in range(9):
                dy, dx = s // 3 - 1, s % 3 - 1
                v = sums[s * GS : (s + 1) * GS, t * CELLS : (t + 1) * CELLS]
                if s != 4:
                    v = pltpu.roll(v, (TW * dy + dx) % CELLS, 1)
                    v = jnp.where(inside(-dy, -dx)[0], v, 0.0)
                out = v if out is None else out + v
            dhb[TILES * e + t] = out
            rsd[TILES * e + t] = rest[:, t * CELLS : (t + 1) * CELLS]
        return 0

    lax.fori_loop(0, FR + 2, back, 0)
    dhb[8:12] = dhb[8:12] + (dhb[0:4] + dhb[4:8])

    def gains(i, acc):
        dact = dhb[pl.ds(8 + 8 * i, 8)] * ds[i]
        dhb[pl.ds(8 + 8 * i, 8)] = dact
        return acc[0] + jnp.sum(dact * xh[i], axis=0), acc[1] + jnp.sum(dact, axis=0)

    dgam, dbet = lax.fori_loop(0, NTM, gains, (zero, zero))
    dgam = jnp.sum(dgam, axis=1, keepdims=True)
    dbet = jnp.sum(dbet, axis=1, keepdims=True)
    m1 = jnp.sum(dbet * gamma, axis=0, keepdims=True) / count
    m2 = jnp.sum(dgam * gamma, axis=0, keepdims=True) / count

    gown[...] = jnp.zeros_like(gown)
    gown[0:1, :] = jnp.sum(jnp.where(diag, dgam * rscale, 0.0), axis=0, keepdims=True)
    gown[1:2, :] = jnp.sum(jnp.where(diag, dbet * rscale, 0.0), axis=0, keepdims=True)
    for r in range(1, NDP):
        to = ahead(d, r, NDP)
        go(gown, gdp.at[d], G_DP + r, {"dp": to})
    gdp[d] = gown[...]

    def dinput(i, _):
        v = inverse * (dhb[pl.ds(8 + 8 * i, 8)] * gamma - m1 - xh[i] * m2)
        dxs[i] = (v + rsd[pl.ds(8 * i, 8)]).astype(BF16)
        return 0

    lax.fori_loop(0, NTM, dinput, 0)
    for r in range(1, NTM):
        zo = ahead(z, r, NTM)
        go(dxs.at[zo], zback.at[z], D_TM + r, {"tm": zo})
    zback[z] = dxs[z]

    for r in range(1, NDP):
        got(drecv.at[behind(d, r, NDP)], D_DP + r)
    acc = drecv[0]
    for i in range(1, NDP):
        acc = acc + drecv[i]
    dsum[...] = acc
    to_owner = copy(dsum, dw_ref, D_OWN, src(d))

    @pl.when(self_t == 0)
    def _():
        to_owner.start()

    @pl.when(self_t == 1)
    def _():
        pltpu.make_async_copy(dsum, dw_ref, recv_sem.at[D_OWN]).start()

    for r in range(1, NDP):
        got(gdp.at[behind(d, r, NDP)], G_DP + r)
    acc = gdp[0]
    for i in range(1, NDP):
        acc = acc + gdp[i]
    gsum[...] = acc
    for r in range(NTM):
        for q in range(NSP):
            if r or q:
                to = {"tm": ahead(z, r, NTM), "space": ahead(y, q, NSP)}
                go(gsum, gall.at[z, y], G_ALL + r * NSP + q, to)
    gall[z, y] = gsum[...]

    for r in range(1, NTM):
        got(zback.at[behind(z, r, NTM)], D_TM + r)
    for t in range(TILES):
        for f in range(2):
            v = zback[:, f * TILES + t].astype(F32).reshape(NTM * GS, CELLS)
            tback[t, f] = v.T.astype(BF16)
    for yo in range(NSP):
        for j in range(CAP):
            tile, live = jnp.int32(0), jnp.int32(0)
            for t in range(TILES):
                here = (owners[t] == yo) & (ranks[t] == j)
                tile, live = jnp.where(here, t, tile), jnp.where(here, 1, live)
            v = tback[tile]
            ysend[yo, :, j] = jnp.where(live > 0, v, jnp.zeros_like(v))
    lanes = pl.ds(pl.multiple_of(y * 128, 128), 128)
    for r in range(1, NSP):
        yo = ahead(y, r, NSP)
        go(ysend.at[yo], dlat_ref.at[:, :, :, lanes], D_SP + r, {"space": yo})
    own = pltpu.make_async_copy(ysend.at[y], dlat_ref.at[:, :, :, lanes], own_sem.at[1])
    own.start()

    for r in range(NTM):
        for q in range(NSP):
            if r or q:
                got(gall.at[behind(z, r, NTM), behind(y, q, NSP)], G_ALL + r * NSP + q)
    for s in range(NSP):
        acc = gall[0, s]
        for i in range(1, NTM):
            acc = acc + gall[i, s]
        dgb_ref[:, s : s + 1, :] = acc[0:2].reshape(2, 1, 128)

    own.wait()
    for r in range(1, NSP):
        yo = behind(y, r, NSP)
        got(dlat_ref.at[:, :, :, pl.ds(pl.multiple_of(yo * 128, 128), 128)], D_SP + r)
    got(dw_ref, D_OWN)
    for c in started:
        c.wait_send()

    @pl.when(self_t == 0)
    def _():
        copy(dsum, dw_ref, D_OWN, src(d)).wait_send()

    @pl.when(jnp.logical_not(w_self))
    def _():
        copy(w_ref, wbuf.at[w_piece], WGT, {"tm": z}).wait_send()


def shards(latents, owner, gamma, beta, weight, upstream):
    vmem = pl.BlockSpec(memory_space=pltpu.VMEM)
    hbm = pl.BlockSpec(memory_space=pl.ANY)
    scratch = [
        ((FR + 4, TILES, CELLS, COUT), BF16),
        ((NSP, 2, CAP, CELLS, 128), BF16),
        ((NTM, 8, GS, CELLS), BF16),
        ((NTM, 8, GS, CELLS), BF16),
        ((8, TAPS, 2, COUT), BF16),
        ((TAPS, GS, COUT), F32),
        ((3, ROWS + GS, COUT), BF16),
        ((ROWS, 512 * (FR + 2)), BF16),
        ((NTM, 8, GS, CELLS), F32),
        ((NTM, 8, GS, CELLS), F32),
        ((TILES * (FR + 2), GS, CELLS), F32),
        ((TILES * (FR + 2), GS, CELLS), F32),
        ((TAPS, GS, COUT), F32),
        ((8, TAPS, 2, COUT), F32),
        ((8, TAPS, 2, COUT), F32),
        ((TAPS, 2, COUT), F32),
        ((NTM, 8, GS, CELLS), BF16),
        ((NTM, 8, GS, CELLS), BF16),
        ((TILES, 2, CELLS, 128), BF16),
        ((NSP, 2, CAP, CELLS, 128), BF16),
        ((8, 128), F32),
        ((NDP, 8, 128), F32),
        ((8, 128), F32),
        ((NTM, NSP, 8, 128), F32),
    ]
    dlat, dw, dgb = pl.pallas_call(
        body,
        out_shape=(
            jax.ShapeDtypeStruct((2, CAP, CELLS, C), BF16),
            jax.ShapeDtypeStruct((TAPS, 2, COUT), F32),
            jax.ShapeDtypeStruct((2, 4, 128), F32),
        ),
        in_specs=[pl.BlockSpec(memory_space=pltpu.SMEM), vmem, vmem, vmem, vmem, vmem],
        out_specs=(hbm, hbm, vmem),
        scratch_shapes=[pltpu.VMEM(s, t) for s, t in scratch]
        + [
            pltpu.SemaphoreType.DMA((N_SEM,)),
            pltpu.SemaphoreType.DMA((N_SEM,)),
            pltpu.SemaphoreType.DMA((2,)),
        ],
        compiler_params=pltpu.CompilerParams(
            collective_id=0, has_side_effects=True, vmem_limit_bytes=56 * 2**20
        ),
    )(
        owner,
        gamma.reshape(4, 128),
        beta.reshape(4, 128),
        latents[0],
        upstream.reshape(2, 4 * CELLS, COUT),
        weight.transpose(1, 0, 2),
    )
    return dlat[None], dw.transpose(1, 0, 2), dgb[0].reshape(C), dgb[1].reshape(C)


def solution(mesh):
    return jax.shard_map(
        shards,
        mesh=mesh,
        in_specs=(
            P("dp", "tm", "space", None, None),
            P("dp", None, None),
            P(),
            P(),
            P(("dp", "tm", "space"), None, None),
            P("dp", "tm", "space", None, None),
        ),
        out_specs=(
            P("dp", "tm", "space", None, None),
            P(("dp", "tm", "space"), None, None),
            P(),
            P(),
        ),
        check_vma=False,
    )
```

```python
import math

import jax
import jax.numpy as jnp
from jax import lax
from jax.experimental import pallas as pl
from jax.experimental.pallas import tpu as pltpu
from jax.sharding import PartitionSpec as P

MESH = pl.DeviceIdType.MESH
F32 = jnp.float32
BF16 = jnp.bfloat16
EPS = 1e-06

NDP, NTM, NSP = 8, 8, 4
GROUPS = 32
GS = 16
FR = 16
TILES = 4
CAP = 2
TH, TW = 8, 16
CELLS = TH * TW
C, COUT = 512, 256
TAPS = 27
ROWS = 9 * GS
LEFT = 48

B_TM, B_SP, A_SP, A_TM = 0, 8, 40, 44
L_SP, L_TM, WGT = 76, 80, 88
D_TM, D_DP, G_DP, D_SP, D_OWN, G_ALL = 96, 112, 120, 128, 136, 137
N_SEM = 169


def body(
    owner_ref, gamma_ref, beta_ref, lat_ref, ups_ref, w_ref,
    dlat_ref, dw_ref, dgam_ref, dbet_ref,
    gz, ybuf, zsend, xbuf, wbuf, wf, wall, a9, xh, ds, dhb, rsd, dk, dsend, drecv, dsum,
    dxs, zback, tback, ysend, gown, gdp, gsum, gall, send_sem, recv_sem, own_sem,
):
    d, z, y = lax.axis_index("dp"), lax.axis_index("tm"), lax.axis_index("space")
    ahead = lambda v, r, n: lax.rem(v + r, n)
    behind = lambda v, r, n: lax.rem(v - r + n, n)
    line = (d * NTM + z) * NSP + y
    mine = y * NTM + z
    w_group = line // 8
    w_tm, w_sp = lax.rem(w_group, NTM), w_group // NTM
    w_piece = lax.rem(line, 8)
    src = lambda i: {
        "dp": mine // 4,
        "tm": 2 * lax.rem(mine, 4) + i // 4,
        "space": lax.rem(jnp.int32(i), 4) if not isinstance(i, int) else i % 4,
    }
    w_self = (w_tm == z) & (w_sp == y)
    own_piece_here = line // 8 == mine

    started = []

    def copy(a, b, n, to, m=None):
        return pltpu.make_async_remote_copy(
            src_ref=a, dst_ref=b, send_sem=send_sem.at[n], recv_sem=recv_sem.at[n if m is None else m],
            device_id=to, device_id_type=MESH,
        )

    def go(a, b, n, to, m=None):
        c = copy(a, b, n, to, m)
        c.start()
        started.append(c)
        return c

    def got(region, n):
        copy(region, region, n, {"tm": z}).wait_recv()

    barrier = pltpu.get_barrier_semaphore()

    def greet(to):
        pl.semaphore_signal(barrier, inc=1, device_id=to, device_id_type=MESH)

    for r in range(NTM):
        for q in range(NSP):
            if r or q:
                greet({"tm": ahead(z, r, NTM), "space": ahead(y, q, NSP)})
    for r in range(1, NDP):
        greet({"dp": ahead(d, r, NDP)})
    for i in range(8):
        o = src(i)

        @pl.when((8 * mine + i) != line)
        def _():
            greet(o)

    @pl.when(jnp.logical_not(own_piece_here & (w_piece == d)))
    def _():
        greet({"dp": w_piece, "tm": w_tm, "space": w_sp})

    p = lax.broadcasted_iota(jnp.int32, (CELLS, 4 * CELLS), 0)
    q = lax.broadcasted_iota(jnp.int32, (CELLS, 4 * CELLS), 1)
    pool = ((q >> 6) == (p >> 4)) & (((q & 31) >> 1) == (p & 15))
    pool = jnp.where(pool, 1.0, 0.0).astype(BF16)
    for f in range(2):
        pooled = jnp.dot(pool, ups_ref[f], preferred_element_type=F32)
        gz[2 * z + f, y] = pooled.astype(BF16)
    dhb[...] = jnp.zeros_like(dhb)
    dk[...] = jnp.zeros_like(dk)

    self_w = jnp.where(w_self, 1, 0)
    self_o = jnp.where(own_piece_here & (w_piece == d), 1, 0)
    self_s = jnp.where(own_piece_here, 1, 0)
    own_to = 8 * mine + d
    self_t = jnp.where(own_to == line, 1, 0)
    pl.semaphore_wait(barrier, NTM * NSP - 1 + NDP - 1 + 8 - self_s + 1 - self_t)

    def part_b(zo, yo, f=0, n=2):
        return gz.at[pl.ds(2 * zo + f, n), yo, pl.ds(LEFT, CELLS - LEFT)]

    def part_a(zo, yo, f=0, n=2):
        return gz.at[pl.ds(2 * zo + f, n), yo, pl.ds(0, LEFT)]

    zr, zl = {"tm": ahead(z, 1, NTM)}, {"tm": behind(z, 1, NTM)}
    yr, yl = {"space": ahead(y, 1, NSP)}, {"space": behind(y, 1, NSP)}
    yo_r, yo_l, yo_2 = ahead(y, 1, NSP), behind(y, 1, NSP), ahead(y, 2, NSP)

    def tm_step(region, base, h):
        frames = (dict(f=0, n=2),) * 2 if h < 4 else (dict(f=0, n=1), dict(f=1, n=1))
        for way, (to, o) in enumerate(((zr, behind(z, h - 1, NTM)), (zl, ahead(z, h - 1, NTM)))):
            a = region(o, **frames[way])
            go(a, a, base + 2 * (h - 1) + way, to)

    def tm_got(region, base, h):
        frames = (dict(f=0, n=2),) * 2 if h < 4 else (dict(f=0, n=1), dict(f=1, n=1))
        for way, o in enumerate((behind(z, h, NTM), ahead(z, h, NTM))):
            got(region(o, **frames[way]), base + 2 * (h - 1) + way)

    def sp_send(region, base, zo):
        a = region(zo, y)
        go(a, a, base, yr)
        go(a, a, base + 1, yl)

    def sp_forward(region, base, zo):
        got(region(zo, yo_l), base)
        a = region(zo, yo_l, 0, 1)
        go(a, a, base + 2, yr)
        got(region(zo, yo_r), base + 1)
        a = region(zo, yo_r, 1, 1)
        go(a, a, base + 3, yl)

    def sp_got(region, base, zo):
        got(region(zo, yo_2, 0, 1), base + 2)
        got(region(zo, yo_2, 1, 1), base + 3)

    steps = (0, -1, 1, -2, 2, -3, 3, 4)
    origin = [lax.rem(z + s + NTM, NTM) for s in steps]
    b_row = lambda zo, yo, f=0, n=2: part_b(zo, yo, f, n)
    b_tm = lambda zo, f=0, n=2: part_b(zo, y, f, n)

    sides = (y, yo_l, yo_r, yo_2)
    a_tm = [lambda zo, f=0, n=2, yo=yo: part_a(zo, yo, f, n) for yo in sides]
    near = [(0,), (1, 2), (3, 4), (5, 6), (7,)]

    def wave(h):
        tm_got(b_tm, B_TM, h)
        if h < 4:
            tm_step(b_tm, B_TM, h + 1)
        for b in near[h]:
            sp_send(b_row, B_SP + 4 * b, origin[b])
        for q in range(4):
            tm_got(a_tm[q], A_TM + 8 * q, h)
            if h < 4:
                tm_step(a_tm[q], A_TM + 8 * q, h + 1)

    def forward(h):
        for b in near[h]:
            sp_forward(b_row, B_SP + 4 * b, origin[b])

    def complete(h):
        for b in near[h]:
            sp_got(b_row, B_SP + 4 * b, origin[b])

    def block(h, i):
        return lax.rem(z + (2 * i - 1) * h + NTM, NTM)

    sp_send(part_a, A_SP, z)
    tm_step(b_tm, B_TM, 1)
    tm_step(a_tm[0], A_TM, 1)
    sp_send(b_row, B_SP, z)

    for r in range(NDP):
        to = {"dp": ahead(d, r, NDP), "tm": w_tm, "space": w_sp}
        c = copy(w_ref, wbuf.at[w_piece], WGT + r, to, WGT + w_piece)
        if r:
            c.start()
            started.append(c)
        else:

            @pl.when(jnp.logical_not(w_self))
            def _():
                c.start()

            @pl.when(w_self)
            def _():
                pltpu.make_async_copy(w_ref, wbuf.at[w_piece], recv_sem.at[WGT + w_piece]).start()

    sp_forward(part_a, A_SP, z)
    tm_step(a_tm[1], A_TM + 8, 1)
    tm_step(a_tm[2], A_TM + 16, 1)

    for r in range(1, NSP):
        yo = ahead(y, r, NSP)
        go(
            lat_ref.at[:, :, :, pl.ds(pl.multiple_of(yo * 128, 128), 128)],
            ybuf.at[y], L_SP + r, {"space": yo},
        )
    own = pltpu.make_async_copy(
        lat_ref.at[:, :, :, pl.ds(pl.multiple_of(y * 128, 128), 128)], ybuf.at[y], own_sem.at[0]
    )
    own.start()

    sp_got(part_a, A_SP, z)
    tm_step(a_tm[3], A_TM + 24, 1)
    wave(1)
    forward(0)

    own.wait()
    for r in range(1, NSP):
        got(ybuf.at[behind(y, r, NSP)], L_SP + r)
    owners = [owner_ref[t] for t in range(TILES)]
    ranks = [
        jnp.minimum(
            sum([(owners[u] == owners[t]).astype(jnp.int32) for u in range(t)], jnp.int32(0)), CAP - 1
        )
        for t in range(TILES)
    ]
    for t in range(TILES):
        for f in range(2):
            v = ybuf[owners[t], f, ranks[t]].astype(F32)
            zsend[:, f * TILES + t] = v.T.reshape(NTM, GS, CELLS).astype(BF16)
    for r in range(1, NTM):
        zo = ahead(z, r, NTM)
        go(zsend.at[zo], xbuf.at[z], L_TM + r, {"tm": zo})
    xbuf[z] = zsend[z]

    for i in range(8):
        got(wbuf.at[i], WGT + i)
    for i in range(8):
        wf[:, 2 * i : 2 * i + 2, :] = wbuf[i].astype(F32)
    wall[0 : 3 * ROWS, :] = wf[...].reshape(3 * ROWS, COUT).astype(BF16)
    pick_r = lax.broadcasted_iota(jnp.int32, (GS, COUT), 0)
    pick_o = lax.broadcasted_iota(jnp.int32, (GS, COUT), 1)
    wall[3 * ROWS : 3 * ROWS + GS, :] = jnp.where(pick_o == mine * GS + pick_r, 1.0, 0.0).astype(BF16)

    cell = lax.broadcasted_iota(jnp.int32, (8, GS, CELLS), 2)
    ix, iy = cell & (TW - 1), cell >> 4

    def inside(dy, dx):
        ok = None
        for cond in (
            [iy + dy >= 0] if dy < 0 else [iy + dy < TH] if dy > 0 else []
        ) + ([ix + dx >= 0] if dx < 0 else [ix + dx < TW] if dx > 0 else []):
            ok = cond if ok is None else ok & cond
        return ok

    nt = (((1,), (1,)), ((), ()))

    def dhidden(h):
        def frame(n, _):
            f = 2 * block(h, n // 2) + lax.rem(n, 2)
            v = lax.dot_general(
                wall[...], gz[f].reshape(TILES * CELLS, COUT), nt, preferred_element_type=F32
            )
            for t in range(TILES):
                lanes = slice(t * CELLS, (t + 1) * CELLS)
                rsd[TILES * f + t] = v[3 * ROWS :, lanes]
                for kt in range(3):
                    out = None
                    for s in range(9):
                        dy, dx = s // 3 - 1, s % 3 - 1
                        w = v[kt * ROWS + s * GS : kt * ROWS + (s + 1) * GS, lanes]
                        if s != 4:
                            w = pltpu.roll(w, (TW * dy + dx) % CELLS, 1)
                            w = jnp.where(inside(-dy, -dx)[0], w, 0.0)
                        out = w if out is None else out + w
                    dhb[TILES * (f + kt) + t] += out
            return 0

        lax.fori_loop(0, 2 * len(near[h]), frame, 0)

    def dweight(h):
        def one(n, _):
            i = block(h, n)
            g = gz[pl.ds(2 * i, 2)].reshape(1024, COUT)
            for kt in range(3):
                a = a9[:, pl.ds(pl.multiple_of(1024 * i + 512 * kt, 512), 1024)]
                dk[9 * kt : 9 * kt + 9] += jnp.dot(a, g, preferred_element_type=F32).reshape(9, GS, COUT)
            return 0

        lax.fori_loop(0, len(near[h]), one, 0)

    wave(2)
    forward(1)
    complete(0)
    dhidden(0)

    wave(3)
    forward(2)

    for r in range(1, NTM):
        got(xbuf.at[behind(z, r, NTM)], L_TM + r)
    count = float(FR * TILES * CELLS * GS)
    zero = jnp.zeros((GS, CELLS), F32)

    def whole(v):
        return jnp.sum(jnp.sum(v, axis=1, keepdims=True), axis=0, keepdims=True)

    def total(i, acc):
        return acc + jnp.sum(xbuf[i].astype(F32), axis=0)

    mean = whole(lax.fori_loop(0, NTM, total, zero)) / count

    def spread(i, acc):
        v = xbuf[i].astype(F32) - mean
        return acc + jnp.sum(v * v, axis=0)

    inverse = lax.rsqrt(whole(lax.fori_loop(0, NTM, spread, zero)) / count + EPS)

    row16 = lax.broadcasted_iota(jnp.int32, (GS, CELLS), 0)
    lane16 = lax.broadcasted_iota(jnp.int32, (GS, CELLS), 1)
    diag = lane16 == z * GS + row16

    def column(ref):
        return jnp.sum(jnp.where(diag, ref[pl.ds(y, 1), :], 0.0), axis=1, keepdims=True)

    gamma, beta = column(gamma_ref), column(beta_ref)

    def taps(i, _):
        normed = (xbuf[i].astype(F32) - mean) * inverse
        act = normed * gamma + beta
        sig = jax.nn.sigmoid(act)
        xh[i] = normed
        ds[i] = sig * (1.0 + act * (1.0 - sig))
        hidden = (act * sig).astype(BF16).astype(F32)
        base = pl.multiple_of((i + 1) * 1024, 1024)
        for s in range(9):
            dy, dx = s // 3 - 1, s % 3 - 1
            v = hidden
            if s != 4:
                v = pltpu.roll(v, (-(TW * dy + dx)) % CELLS, 2)
                v = jnp.where(inside(dy, dx), v, 0.0)
            v = v.astype(BF16)
            for j in range(8):
                a9[s * GS : (s + 1) * GS, pl.ds(base + j * CELLS, CELLS)] = v[j]
        return 0

    lax.fori_loop(0, NTM, taps, 0)
    a9[:, 0:512] = a9[:, 1024:1536]
    a9[:, 512:1024] = a9[:, 1024:1536]

    complete(1)
    dhidden(1)

    wave(4)
    forward(3)
    complete(2)
    dhidden(2)
    forward(4)
    dweight(0)
    dweight(1)
    dweight(2)
    complete(3)
    dhidden(3)
    dweight(3)
    complete(4)
    dweight(4)

    rscale = 1.0 / math.sqrt(NDP * FR * TILES * CELLS)
    for i in range(8):
        dsend[i] = dk[:, 2 * i : 2 * i + 2, :] * rscale
    for r in range(1, NDP):
        to = ahead(d, r, NDP)
        go(dsend.at[to], drecv.at[d], D_DP + r, {"dp": to})
    drecv[d] = dsend[d]

    dhidden(4)
    dhb[8:12] = dhb[8:12] + (dhb[0:4] + dhb[4:8])

    def gains(i, acc):
        dact = dhb[pl.ds(8 + 8 * i, 8)] * ds[i]
        dhb[pl.ds(8 + 8 * i, 8)] = dact
        return acc[0] + jnp.sum(dact * xh[i], axis=0), acc[1] + jnp.sum(dact, axis=0)

    dgam, dbet = lax.fori_loop(0, NTM, gains, (zero, zero))
    dgam = jnp.sum(dgam, axis=1, keepdims=True)
    dbet = jnp.sum(dbet, axis=1, keepdims=True)
    m1 = jnp.sum(dbet * gamma, axis=0, keepdims=True) / count
    m2 = jnp.sum(dgam * gamma, axis=0, keepdims=True) / count

    def dinput(i, _):
        v = inverse * (dhb[pl.ds(8 + 8 * i, 8)] * gamma - m1 - xh[i] * m2)
        dxs[i] = (v + rsd[pl.ds(8 * i, 8)]).astype(BF16)
        return 0

    lax.fori_loop(0, NTM, dinput, 0)

    def of_frame(ref, i, f):
        return ref.at[i, pl.ds(f * TILES, TILES)]

    for f in range(2):
        for r in range(1, NTM):
            zo = ahead(z, r, NTM)
            go(of_frame(dxs, zo, f), of_frame(zback, z, f), D_TM + 8 * f + r, {"tm": zo})
    zback[z] = dxs[z]

    gown[...] = jnp.zeros_like(gown)
    gown[0:1, :] = jnp.sum(jnp.where(diag, dgam * rscale, 0.0), axis=0, keepdims=True)
    gown[1:2, :] = jnp.sum(jnp.where(diag, dbet * rscale, 0.0), axis=0, keepdims=True)
    for r in range(1, NDP):
        to = ahead(d, r, NDP)
        go(gown, gdp.at[d], G_DP + r, {"dp": to})
    gdp[d] = gown[...]

    lanes = pl.ds(pl.multiple_of(y * 128, 128), 128)

    def to_slots(f):
        for r in range(1, NTM):
            got(of_frame(zback, behind(z, r, NTM), f), D_TM + 8 * f + r)
        for t in range(TILES):
            v = zback[:, f * TILES + t].astype(F32).reshape(NTM * GS, CELLS)
            tback[f, t] = v.T.astype(BF16)
        for yo in range(NSP):
            for j in range(CAP):
                tile, live = jnp.int32(0), jnp.int32(0)
                for t in range(TILES):
                    here = (owners[t] == yo) & (ranks[t] == j)
                    tile, live = jnp.where(here, t, tile), jnp.where(here, 1, live)
                v = tback[f, tile]
                ysend[f, yo, j] = jnp.where(live > 0, v, jnp.zeros_like(v))
        for r in range(1, NSP):
            yo = ahead(y, r, NSP)
            go(ysend.at[f, yo], dlat_ref.at[f, :, :, lanes], D_SP + 4 * f + r, {"space": yo})
        own = pltpu.make_async_copy(ysend.at[f, y], dlat_ref.at[f, :, :, lanes], own_sem.at[1 + f])
        own.start()
        return own

    owns = [to_slots(0)]

    for r in range(1, NDP):
        got(gdp.at[behind(d, r, NDP)], G_DP + r)
    acc = gdp[0]
    for i in range(1, NDP):
        acc = acc + gdp[i]
    gsum[...] = acc
    for r in range(NTM):
        for q in range(NSP):
            if r or q:
                to = {"tm": ahead(z, r, NTM), "space": ahead(y, q, NSP)}
                go(gsum, gall.at[z, y], G_ALL + r * NSP + q, to)
    gall[z, y] = gsum[...]

    owns.append(to_slots(1))

    for r in range(1, NDP):
        got(drecv.at[behind(d, r, NDP)], D_DP + r)
    acc = drecv[0]
    for i in range(1, NDP):
        acc = acc + drecv[i]
    dsum[...] = acc
    to_owner = copy(dsum, dw_ref, D_OWN, src(d))

    @pl.when(self_t == 0)
    def _():
        to_owner.start()

    @pl.when(self_t == 1)
    def _():
        pltpu.make_async_copy(dsum, dw_ref, recv_sem.at[D_OWN]).start()

    for r in range(NTM):
        for q in range(NSP):
            if r or q:
                got(gall.at[behind(z, r, NTM), behind(y, q, NSP)], G_ALL + r * NSP + q)
    for s in range(NSP):
        acc = gall[0, s]
        for i in range(1, NTM):
            acc = acc + gall[i, s]
        dgam_ref[s : s + 1, :] = acc[0:1]
        dbet_ref[s : s + 1, :] = acc[1:2]

    for f in range(2):
        owns[f].wait()
        for r in range(1, NSP):
            yo = behind(y, r, NSP)
            got(dlat_ref.at[f, :, :, pl.ds(pl.multiple_of(yo * 128, 128), 128)], D_SP + 4 * f + r)
    got(dw_ref, D_OWN)
    for c in started:
        c.wait_send()

    @pl.when(self_t == 0)
    def _():
        copy(dsum, dw_ref, D_OWN, src(d)).wait_send()

    @pl.when(jnp.logical_not(w_self))
    def _():
        copy(w_ref, wbuf.at[w_piece], WGT, {"tm": z}).wait_send()


def shards(latents, owner, gamma, beta, weight, upstream):
    vmem = pl.BlockSpec(memory_space=pltpu.VMEM)
    hbm = pl.BlockSpec(memory_space=pl.ANY)
    scratch = [
        ((FR, TILES, CELLS, COUT), BF16),
        ((NSP, 2, CAP, CELLS, 128), BF16),
        ((NTM, 8, GS, CELLS), BF16),
        ((NTM, 8, GS, CELLS), BF16),
        ((8, TAPS, 2, COUT), BF16),
        ((TAPS, GS, COUT), F32),
        ((3 * ROWS + GS, COUT), BF16),
        ((ROWS, 512 * (FR + 2)), BF16),
        ((NTM, 8, GS, CELLS), F32),
        ((NTM, 8, GS, CELLS), F32),
        ((TILES * (FR + 2), GS, CELLS), F32),
        ((TILES * FR, GS, CELLS), F32),
        ((TAPS, GS, COUT), F32),
        ((8, TAPS, 2, COUT), F32),
        ((8, TAPS, 2, COUT), F32),
        ((TAPS, 2, COUT), F32),
        ((NTM, 8, GS, CELLS), BF16),
        ((NTM, 8, GS, CELLS), BF16),
        ((2, TILES, CELLS, 128), BF16),
        ((2, NSP, CAP, CELLS, 128), BF16),
        ((8, 128), F32),
        ((NDP, 8, 128), F32),
        ((8, 128), F32),
        ((NTM, NSP, 8, 128), F32),
    ]
    dlat, dw, dgam, dbet = pl.pallas_call(
        body,
        out_shape=(
            jax.ShapeDtypeStruct((2, CAP, CELLS, C), BF16),
            jax.ShapeDtypeStruct((TAPS, 2, COUT), F32),
            jax.ShapeDtypeStruct((4, 128), F32),
            jax.ShapeDtypeStruct((4, 128), F32),
        ),
        in_specs=[pl.BlockSpec(memory_space=pltpu.SMEM), vmem, vmem, vmem, vmem, vmem],
        out_specs=(hbm, hbm, vmem, vmem),
        scratch_shapes=[pltpu.VMEM(s, t) for s, t in scratch]
        + [
            pltpu.SemaphoreType.DMA((N_SEM,)),
            pltpu.SemaphoreType.DMA((N_SEM,)),
            pltpu.SemaphoreType.DMA((3,)),
        ],
        compiler_params=pltpu.CompilerParams(
            collective_id=0, has_side_effects=True, vmem_limit_bytes=56 * 2**20
        ),
    )(
        owner.reshape(TILES),
        gamma.reshape(4, 128),
        beta.reshape(4, 128),
        latents[0],
        upstream.reshape(2, 4 * CELLS, COUT),
        weight.transpose(1, 0, 2),
    )
    return dlat[None], dw.transpose(1, 0, 2), dgam.reshape(C), dbet.reshape(C)


def solution(mesh):
    return jax.shard_map(
        shards,
        mesh=mesh,
        in_specs=(
            P("dp", "tm", "space", None, None),
            P("dp", None, None),
            P(),
            P(),
            P(("dp", "tm", "space"), None, None),
            P("dp", "tm", "space", None, None),
        ),
        out_specs=(
            P("dp", "tm", "space", None, None),
            P(("dp", "tm", "space"), None, None),
            P(),
            P(),
        ),
        check_vma=False,
    )
```

```python
import math

import jax
import jax.numpy as jnp
from jax import lax
from jax.experimental import pallas as pl
from jax.experimental.pallas import tpu as pltpu
from jax.sharding import PartitionSpec as P

MESH = pl.DeviceIdType.MESH
F32 = jnp.float32
BF16 = jnp.bfloat16
EPS = 1e-06

NDP, NTM, NSP = 8, 8, 4
GROUPS = 32
GS = 16
FR = 16
TILES = 4
CAP = 2
TH, TW = 8, 16
CELLS = TH * TW
C, COUT = 512, 256
TAPS = 27
ROWS = 9 * GS
LEFT = 48

B_TM, B_SP, A_SP, A_TM = 0, 8, 40, 44
L_SP, L_TM, WGT = 76, 80, 88
D_TM, D_DP, G_DP, D_SP, D_OWN, G_ALL = 112, 128, 136, 144, 152, 153
N_SEM = 185


def body(
    owner_ref, gamma_ref, beta_ref, lat_ref, ups_ref, w_ref,
    dlat_ref, dw_ref, dgam_ref, dbet_ref,
    gz, ybuf, zsend, xbuf, wbuf, wf, wall, a9, xh, ds, dhb, rsd, dk, dsend, drecv, dsum,
    dxs, zback, tback, ysend, gown, gdp, gsum, gall, send_sem, recv_sem, own_sem,
):
    d, z, y = lax.axis_index("dp"), lax.axis_index("tm"), lax.axis_index("space")
    ahead = lambda v, r, n: lax.rem(v + r, n)
    behind = lambda v, r, n: lax.rem(v - r + n, n)
    line = (d * NTM + z) * NSP + y
    mine = y * NTM + z
    w_group = line // 8
    w_tm, w_sp = lax.rem(w_group, NTM), w_group // NTM
    w_piece = lax.rem(line, 8)
    src = lambda i: {
        "dp": mine // 4,
        "tm": 2 * lax.rem(mine, 4) + i // 4,
        "space": lax.rem(jnp.int32(i), 4) if not isinstance(i, int) else i % 4,
    }
    w_self = (w_tm == z) & (w_sp == y)
    w_home = d == mine // 4
    own_piece_here = line // 8 == mine

    started = []

    def copy(a, b, n, to, m=None):
        return pltpu.make_async_remote_copy(
            src_ref=a, dst_ref=b, send_sem=send_sem.at[n], recv_sem=recv_sem.at[n if m is None else m],
            device_id=to, device_id_type=MESH,
        )

    def go(a, b, n, to, m=None):
        c = copy(a, b, n, to, m)
        c.start()
        started.append(c)
        return c

    def got(region, n):
        copy(region, region, n, {"tm": z}).wait_recv()

    barrier = pltpu.get_barrier_semaphore()

    def greet(to):
        pl.semaphore_signal(barrier, inc=1, device_id=to, device_id_type=MESH)

    for r in range(NTM):
        for q in range(NSP):
            if r or q:
                greet({"tm": ahead(z, r, NTM), "space": ahead(y, q, NSP)})
    for r in range(1, NDP):
        greet({"dp": ahead(d, r, NDP)})
    @pl.when(jnp.logical_not(own_piece_here & (w_piece == d)))
    def _():
        greet({"dp": w_piece, "tm": w_tm, "space": w_sp})

    p = lax.broadcasted_iota(jnp.int32, (CELLS, 4 * CELLS), 0)
    q = lax.broadcasted_iota(jnp.int32, (CELLS, 4 * CELLS), 1)
    pool = ((q >> 6) == (p >> 4)) & (((q & 31) >> 1) == (p & 15))
    pool = jnp.where(pool, 1.0, 0.0).astype(BF16)
    for f in range(2):
        pooled = jnp.dot(pool, ups_ref[f], preferred_element_type=F32)
        gz[2 * z + f, y] = pooled.astype(BF16)
    dhb[...] = jnp.zeros_like(dhb)
    dk[...] = jnp.zeros_like(dk)

    own_to = 8 * mine + d
    self_t = jnp.where(own_to == line, 1, 0)
    pl.semaphore_wait(barrier, NTM * NSP - 1 + NDP - 1 + 1 - self_t)

    def part_b(zo, yo, f=0, n=2):
        return gz.at[pl.ds(2 * zo + f, n), yo, pl.ds(LEFT, CELLS - LEFT)]

    def part_a(zo, yo, f=0, n=2):
        return gz.at[pl.ds(2 * zo + f, n), yo, pl.ds(0, LEFT)]

    zr, zl = {"tm": ahead(z, 1, NTM)}, {"tm": behind(z, 1, NTM)}
    yr, yl = {"space": ahead(y, 1, NSP)}, {"space": behind(y, 1, NSP)}
    yo_r, yo_l, yo_2 = ahead(y, 1, NSP), behind(y, 1, NSP), ahead(y, 2, NSP)

    def tm_step(region, base, h):
        frames = (dict(f=0, n=2),) * 2 if h < 4 else (dict(f=0, n=1), dict(f=1, n=1))
        for way, (to, o) in enumerate(((zr, behind(z, h - 1, NTM)), (zl, ahead(z, h - 1, NTM)))):
            a = region(o, **frames[way])
            go(a, a, base + 2 * (h - 1) + way, to)

    def tm_got(region, base, h):
        frames = (dict(f=0, n=2),) * 2 if h < 4 else (dict(f=0, n=1), dict(f=1, n=1))
        for way, o in enumerate((behind(z, h, NTM), ahead(z, h, NTM))):
            got(region(o, **frames[way]), base + 2 * (h - 1) + way)

    def sp_send(region, base, zo):
        a = region(zo, y)
        go(a, a, base, yr)
        go(a, a, base + 1, yl)

    def sp_forward(region, base, zo):
        got(region(zo, yo_l), base)
        a = region(zo, yo_l, 0, 1)
        go(a, a, base + 2, yr)
        got(region(zo, yo_r), base + 1)
        a = region(zo, yo_r, 1, 1)
        go(a, a, base + 3, yl)

    def sp_got(region, base, zo):
        got(region(zo, yo_2, 0, 1), base + 2)
        got(region(zo, yo_2, 1, 1), base + 3)

    steps = (0, -1, 1, -2, 2, -3, 3, 4)
    origin = [lax.rem(z + s + NTM, NTM) for s in steps]
    b_row = lambda zo, yo, f=0, n=2: part_b(zo, yo, f, n)
    b_tm = lambda zo, f=0, n=2: part_b(zo, y, f, n)

    sides = (y, yo_l, yo_r, yo_2)
    a_tm = [lambda zo, f=0, n=2, yo=yo: part_a(zo, yo, f, n) for yo in sides]
    near = [(0,), (1, 2), (3, 4), (5, 6), (7,)]

    def wave_b(h):
        tm_got(b_tm, B_TM, h)
        if h < 4:
            tm_step(b_tm, B_TM, h + 1)
        for b in near[h]:
            sp_send(b_row, B_SP + 4 * b, origin[b])

    def wave_a(h):
        for q in range(4):
            tm_got(a_tm[q], A_TM + 8 * q, h)
            if h < 4:
                tm_step(a_tm[q], A_TM + 8 * q, h + 1)

    def forward(h):
        for b in near[h]:
            sp_forward(b_row, B_SP + 4 * b, origin[b])

    def complete(h):
        for b in near[h]:
            sp_got(b_row, B_SP + 4 * b, origin[b])

    def block(h, i):
        return lax.rem(z + (2 * i - 1) * h + NTM, NTM)

    cell = lax.broadcasted_iota(jnp.int32, (8, GS, CELLS), 2)
    ix, iy = cell & (TW - 1), cell >> 4

    def inside(dy, dx):
        ok = None
        for cond in (
            [iy + dy >= 0] if dy < 0 else [iy + dy < TH] if dy > 0 else []
        ) + ([ix + dx >= 0] if dx < 0 else [ix + dx < TW] if dx > 0 else []):
            ok = cond if ok is None else ok & cond
        return ok

    nt = (((1,), (1,)), ((), ()))

    def dhidden(h):
        def frame(n, _):
            f = 2 * block(h, n // 2) + lax.rem(n, 2)
            v = lax.dot_general(
                wall[...], gz[f].reshape(TILES * CELLS, COUT), nt, preferred_element_type=F32
            )
            for t in range(TILES):
                lanes = slice(t * CELLS, (t + 1) * CELLS)
                rsd[TILES * f + t] = v[3 * ROWS :, lanes]
                for kt in range(3):
                    out = None
                    for s in range(9):
                        dy, dx = s // 3 - 1, s % 3 - 1
                        w = v[kt * ROWS + s * GS : kt * ROWS + (s + 1) * GS, lanes]
                        if s != 4:
                            w = pltpu.roll(w, (TW * dy + dx) % CELLS, 1)
                            w = jnp.where(inside(-dy, -dx)[0], w, 0.0)
                        out = w if out is None else out + w
                    dhb[TILES * (f + kt) + t] += out
            return 0

        lax.fori_loop(0, 2 * len(near[h]), frame, 0)

    def dweight(h):
        def one(n, _):
            i = block(h, n)
            g = gz[pl.ds(2 * i, 2)].reshape(1024, COUT)
            for kt in range(3):
                a = a9[:, pl.ds(pl.multiple_of(1024 * i + 512 * kt, 512), 1024)]
                dk[9 * kt : 9 * kt + 9] += jnp.dot(a, g, preferred_element_type=F32).reshape(9, GS, COUT)
            return 0

        lax.fori_loop(0, len(near[h]), one, 0)

    sp_send(part_a, A_SP, z)
    tm_step(b_tm, B_TM, 1)
    sp_send(b_row, B_SP, z)

    to_group = copy(w_ref, wbuf.at[w_piece], WGT + 8, {"tm": w_tm, "space": w_sp}, WGT + w_piece)

    @pl.when(jnp.logical_not(w_self))
    def _():
        to_group.start()

    @pl.when(w_self)
    def _():
        pltpu.make_async_copy(w_ref, wbuf.at[w_piece], recv_sem.at[WGT + w_piece]).start()

    wave_b(1)
    sp_forward(part_a, A_SP, z)
    for q in range(3):
        tm_step(a_tm[q], A_TM + 8 * q, 1)
    wave_b(2)

    for r in range(1, NSP):
        yo = ahead(y, r, NSP)
        go(
            lat_ref.at[:, :, :, pl.ds(pl.multiple_of(yo * 128, 128), 128)],
            ybuf.at[y], L_SP + r, {"space": yo},
        )
    own = pltpu.make_async_copy(
        lat_ref.at[:, :, :, pl.ds(pl.multiple_of(y * 128, 128), 128)], ybuf.at[y], own_sem.at[0]
    )
    own.start()

    sp_got(part_a, A_SP, z)
    tm_step(a_tm[3], A_TM + 24, 1)
    forward(0)

    @pl.when(w_home)
    def _():
        for i in range(8):
            got(wbuf.at[i], WGT + i)
        for r in range(1, NDP):
            copy(wbuf, wbuf, WGT + 9 + r, {"dp": ahead(d, r, NDP)}, WGT + 9).start()

    wave_b(3)
    wave_a(1)
    wave_b(4)

    own.wait()
    for r in range(1, NSP):
        got(ybuf.at[behind(y, r, NSP)], L_SP + r)
    owners = [owner_ref[t] for t in range(TILES)]
    ranks = [
        jnp.minimum(
            sum([(owners[u] == owners[t]).astype(jnp.int32) for u in range(t)], jnp.int32(0)), CAP - 1
        )
        for t in range(TILES)
    ]
    for t in range(TILES):
        for f in range(2):
            v = ybuf[owners[t], f, ranks[t]].astype(F32)
            zsend[:, f * TILES + t] = v.T.reshape(NTM, GS, CELLS).astype(BF16)
    for r in range(1, NTM):
        zo = ahead(z, r, NTM)
        go(zsend.at[zo], xbuf.at[z], L_TM + r, {"tm": zo})
    xbuf[z] = zsend[z]

    @pl.when(jnp.logical_not(w_home))
    def _():
        got(wbuf, WGT + 9)

    for i in range(8):
        wf[:, 2 * i : 2 * i + 2, :] = wbuf[i].astype(F32)
    wall[0 : 3 * ROWS, :] = wf[...].reshape(3 * ROWS, COUT).astype(BF16)
    pick_r = lax.broadcasted_iota(jnp.int32, (GS, COUT), 0)
    pick_o = lax.broadcasted_iota(jnp.int32, (GS, COUT), 1)
    wall[3 * ROWS : 3 * ROWS + GS, :] = jnp.where(pick_o == mine * GS + pick_r, 1.0, 0.0).astype(BF16)

    forward(1)
    complete(0)
    dhidden(0)
    wave_a(2)
    forward(2)
    complete(1)
    dhidden(1)

    for r in range(1, NTM):
        got(xbuf.at[behind(z, r, NTM)], L_TM + r)
    count = float(FR * TILES * CELLS * GS)
    zero = jnp.zeros((GS, CELLS), F32)

    def whole(v):
        return jnp.sum(jnp.sum(v, axis=1, keepdims=True), axis=0, keepdims=True)

    def total(i, acc):
        return acc + jnp.sum(xbuf[i].astype(F32), axis=0)

    mean = whole(lax.fori_loop(0, NTM, total, zero)) / count

    def spread(i, acc):
        v = xbuf[i].astype(F32) - mean
        return acc + jnp.sum(v * v, axis=0)

    inverse = lax.rsqrt(whole(lax.fori_loop(0, NTM, spread, zero)) / count + EPS)

    row16 = lax.broadcasted_iota(jnp.int32, (GS, CELLS), 0)
    lane16 = lax.broadcasted_iota(jnp.int32, (GS, CELLS), 1)
    diag = lane16 == z * GS + row16

    def column(ref):
        return jnp.sum(jnp.where(diag, ref[pl.ds(y, 1), :], 0.0), axis=1, keepdims=True)

    gamma, beta = column(gamma_ref), column(beta_ref)

    def taps(i, _):
        normed = (xbuf[i].astype(F32) - mean) * inverse
        act = normed * gamma + beta
        sig = jax.nn.sigmoid(act)
        xh[i] = normed
        ds[i] = sig * (1.0 + act * (1.0 - sig))
        hidden = (act * sig).astype(BF16).astype(F32)
        base = pl.multiple_of((i + 1) * 1024, 1024)
        for s in range(9):
            dy, dx = s // 3 - 1, s % 3 - 1
            v = hidden
            if s != 4:
                v = pltpu.roll(v, (-(TW * dy + dx)) % CELLS, 2)
                v = jnp.where(inside(dy, dx), v, 0.0)
            v = v.astype(BF16)
            for j in range(8):
                a9[s * GS : (s + 1) * GS, pl.ds(base + j * CELLS, CELLS)] = v[j]
        return 0

    lax.fori_loop(0, NTM, taps, 0)
    a9[:, 0:512] = a9[:, 1024:1536]
    a9[:, 512:1024] = a9[:, 1024:1536]

    wave_a(3)
    forward(3)
    dweight(0)
    dweight(1)
    complete(2)
    dhidden(2)
    dweight(2)
    forward(4)
    complete(3)
    dhidden(3)
    dweight(3)
    wave_a(4)
    complete(4)
    dweight(4)

    rscale = 1.0 / math.sqrt(NDP * FR * TILES * CELLS)
    for i in range(8):
        dsend[i] = dk[:, 2 * i : 2 * i + 2, :] * rscale
    for r in range(1, NDP):
        to = ahead(d, r, NDP)
        go(dsend.at[to], drecv.at[d], D_DP + r, {"dp": to})
    drecv[d] = dsend[d]

    dhidden(4)
    dhb[8:12] = dhb[8:12] + (dhb[0:4] + dhb[4:8])

    def gains(i, acc):
        dact = dhb[pl.ds(8 + 8 * i, 8)] * ds[i]
        dhb[pl.ds(8 + 8 * i, 8)] = dact
        return acc[0] + jnp.sum(dact * xh[i], axis=0), acc[1] + jnp.sum(dact, axis=0)

    dgam, dbet = lax.fori_loop(0, NTM, gains, (zero, zero))
    dgam = jnp.sum(dgam, axis=1, keepdims=True)
    dbet = jnp.sum(dbet, axis=1, keepdims=True)
    m1 = jnp.sum(dbet * gamma, axis=0, keepdims=True) / count
    m2 = jnp.sum(dgam * gamma, axis=0, keepdims=True) / count

    def dinput(i, _):
        v = inverse * (dhb[pl.ds(8 + 8 * i, 8)] * gamma - m1 - xh[i] * m2)
        dxs[i] = (v + rsd[pl.ds(8 * i, 8)]).astype(BF16)
        return 0

    lax.fori_loop(0, NTM, dinput, 0)

    def of_frame(ref, i, f):
        return ref.at[i, pl.ds(f * TILES, TILES)]

    for f in range(2):
        for r in range(1, NTM):
            zo = ahead(z, r, NTM)
            go(of_frame(dxs, zo, f), of_frame(zback, z, f), D_TM + 8 * f + r, {"tm": zo})
    zback[z] = dxs[z]

    gown[0:1, :] = jnp.sum(jnp.where(diag, dgam * rscale, 0.0), axis=0, keepdims=True)
    gown[1:2, :] = jnp.sum(jnp.where(diag, dbet * rscale, 0.0), axis=0, keepdims=True)
    for r in range(1, NDP):
        to = ahead(d, r, NDP)
        go(gown, gdp.at[d], G_DP + r, {"dp": to})
    gdp[d] = gown[...]

    lanes = pl.ds(pl.multiple_of(y * 128, 128), 128)

    def to_slots(f):
        for r in range(1, NTM):
            got(of_frame(zback, behind(z, r, NTM), f), D_TM + 8 * f + r)
        for t in range(TILES):
            v = zback[:, f * TILES + t].astype(F32).reshape(NTM * GS, CELLS)
            tback[f, t] = v.T.astype(BF16)
        for yo in range(NSP):
            for j in range(CAP):
                tile, live = jnp.int32(0), jnp.int32(0)
                for t in range(TILES):
                    here = (owners[t] == yo) & (ranks[t] == j)
                    tile, live = jnp.where(here, t, tile), jnp.where(here, 1, live)
                v = tback[f, tile]
                ysend[f, yo, j] = jnp.where(live > 0, v, jnp.zeros_like(v))
        for r in range(1, NSP):
            yo = ahead(y, r, NSP)
            go(ysend.at[f, yo], dlat_ref.at[f, :, :, lanes], D_SP + 4 * f + r, {"space": yo})
        own = pltpu.make_async_copy(ysend.at[f, y], dlat_ref.at[f, :, :, lanes], own_sem.at[1 + f])
        own.start()
        return own

    owns = [to_slots(0)]

    for r in range(1, NDP):
        got(gdp.at[behind(d, r, NDP)], G_DP + r)
    acc = gdp[0]
    for i in range(1, NDP):
        acc = acc + gdp[i]
    gsum[...] = acc
    for r in range(NTM):
        for q in range(NSP):
            if r or q:
                to = {"tm": ahead(z, r, NTM), "space": ahead(y, q, NSP)}
                go(gsum, gall.at[z, y], G_ALL + r * NSP + q, to)
    gall[z, y] = gsum[...]

    owns.append(to_slots(1))

    for r in range(1, NDP):
        got(drecv.at[behind(d, r, NDP)], D_DP + r)
    acc = drecv[0]
    for i in range(1, NDP):
        acc = acc + drecv[i]
    dsum[...] = acc
    to_owner = copy(dsum, dw_ref, D_OWN, src(d))

    @pl.when(self_t == 0)
    def _():
        to_owner.start()

    @pl.when(self_t == 1)
    def _():
        pltpu.make_async_copy(dsum, dw_ref, recv_sem.at[D_OWN]).start()

    for r in range(NTM):
        for q in range(NSP):
            if r or q:
                got(gall.at[behind(z, r, NTM), behind(y, q, NSP)], G_ALL + r * NSP + q)
    for s in range(NSP):
        acc = gall[0, s]
        for i in range(1, NTM):
            acc = acc + gall[i, s]
        dgam_ref[s : s + 1, :] = acc[0:1]
        dbet_ref[s : s + 1, :] = acc[1:2]

    for f in range(2):
        owns[f].wait()
        for r in range(1, NSP):
            yo = behind(y, r, NSP)
            got(dlat_ref.at[f, :, :, pl.ds(pl.multiple_of(yo * 128, 128), 128)], D_SP + 4 * f + r)
    got(dw_ref, D_OWN)
    for c in started:
        c.wait_send()

    @pl.when(self_t == 0)
    def _():
        copy(dsum, dw_ref, D_OWN, src(d)).wait_send()

    @pl.when(jnp.logical_not(w_self))
    def _():
        copy(w_ref, wbuf.at[w_piece], WGT + 8, {"tm": z}).wait_send()

    @pl.when(w_home)
    def _():
        for r in range(1, NDP):
            copy(wbuf, wbuf, WGT + 9 + r, {"dp": ahead(d, r, NDP)}, WGT + 9).wait_send()


def shards(latents, owner, gamma, beta, weight, upstream):
    vmem = pl.BlockSpec(memory_space=pltpu.VMEM)
    hbm = pl.BlockSpec(memory_space=pl.ANY)
    scratch = [
        ((FR, TILES, CELLS, COUT), BF16),
        ((NSP, 2, CAP, CELLS, 128), BF16),
        ((NTM, 8, GS, CELLS), BF16),
        ((NTM, 8, GS, CELLS), BF16),
        ((8, TAPS, 2, COUT), BF16),
        ((TAPS, GS, COUT), F32),
        ((3 * ROWS + GS, COUT), BF16),
        ((ROWS, 512 * (FR + 2)), BF16),
        ((NTM, 8, GS, CELLS), F32),
        ((NTM, 8, GS, CELLS), F32),
        ((TILES * (FR + 2), GS, CELLS), F32),
        ((TILES * FR, GS, CELLS), F32),
        ((TAPS, GS, COUT), F32),
        ((8, TAPS, 2, COUT), F32),
        ((8, TAPS, 2, COUT), F32),
        ((TAPS, 2, COUT), F32),
        ((NTM, 8, GS, CELLS), BF16),
        ((NTM, 8, GS, CELLS), BF16),
        ((2, TILES, CELLS, 128), BF16),
        ((2, NSP, CAP, CELLS, 128), BF16),
        ((2, 128), F32),
        ((NDP, 2, 128), F32),
        ((2, 128), F32),
        ((NTM, NSP, 2, 128), F32),
    ]
    dlat, dw, dgam, dbet = pl.pallas_call(
        body,
        out_shape=(
            jax.ShapeDtypeStruct((2, CAP, CELLS, C), BF16),
            jax.ShapeDtypeStruct((TAPS, 2, COUT), F32),
            jax.ShapeDtypeStruct((4, 128), F32),
            jax.ShapeDtypeStruct((4, 128), F32),
        ),
        in_specs=[pl.BlockSpec(memory_space=pltpu.SMEM), vmem, vmem, vmem, vmem, vmem],
        out_specs=(hbm, hbm, vmem, vmem),
        scratch_shapes=[pltpu.VMEM(s, t) for s, t in scratch]
        + [
            pltpu.SemaphoreType.DMA((N_SEM,)),
            pltpu.SemaphoreType.DMA((N_SEM,)),
            pltpu.SemaphoreType.DMA((3,)),
        ],
        compiler_params=pltpu.CompilerParams(
            collective_id=0, has_side_effects=True, vmem_limit_bytes=56 * 2**20
        ),
    )(
        owner.reshape(TILES),
        gamma.reshape(4, 128),
        beta.reshape(4, 128),
        latents[0],
        upstream.reshape(2, 4 * CELLS, COUT),
        weight.transpose(1, 0, 2),
    )
    return dlat[None], dw.transpose(1, 0, 2), dgam.reshape(C), dbet.reshape(C)


def solution(mesh):
    return jax.shard_map(
        shards,
        mesh=mesh,
        in_specs=(
            P("dp", "tm", "space", None, None),
            P("dp", None, None),
            P(),
            P(),
            P(("dp", "tm", "space"), None, None),
            P("dp", "tm", "space", None, None),
        ),
        out_specs=(
            P("dp", "tm", "space", None, None),
            P(("dp", "tm", "space"), None, None),
            P(),
            P(),
        ),
        check_vma=False,
    )
```

```python
import math

import jax
import jax.numpy as jnp
from jax import lax
from jax.experimental import pallas as pl
from jax.experimental.pallas import tpu as pltpu
from jax.sharding import PartitionSpec as P

MESH = pl.DeviceIdType.MESH
F32 = jnp.float32
BF16 = jnp.bfloat16
EPS = 1e-06

NDP, NTM, NSP = 8, 8, 4
GROUPS = 32
GS = 16
FR = 16
TILES = 4
CAP = 2
TH, TW = 8, 16
CELLS = TH * TW
C, COUT = 512, 256
TAPS = 27
ROWS = 9 * GS
LEFT = 48

B_TM, B_SP, A_SP, A_TM = 0, 8, 40, 44
L_SP, L_TM, WGT = 76, 80, 88
D_TM, D_DP, G_DP, D_SP, D_OWN, G_ALL = 112, 128, 136, 144, 152, 153
N_SEM = 185


def body(
    owner_ref, gamma_ref, beta_ref, lat_ref, ups_ref, w_ref,
    dlat_ref, dw_ref, dgam_ref, dbet_ref,
    gz, ybuf, zsend, xbuf, wbuf, wf, wall, a9, xh, ds, dhb, rsd, dk, dsend, drecv, dsum,
    dxs, zback, tback, ysend, gown, gdp, gsum, gall, send_sem, recv_sem, own_sem,
):
    d, z, y = lax.axis_index("dp"), lax.axis_index("tm"), lax.axis_index("space")
    ahead = lambda v, r, n: lax.rem(v + r, n)
    behind = lambda v, r, n: lax.rem(v - r + n, n)
    line = (d * NTM + z) * NSP + y
    place = lambda v: 4 * lax.rem(v, 2) + v // 2
    tz = place(z)
    mine = y * NTM + tz
    w_group = line // 8
    w_tm, w_sp = 2 * lax.rem(w_group, 4) + lax.rem(w_group, NTM) // 4, w_group // NTM
    w_piece = lax.rem(line, 8)
    src = lambda i: {
        "dp": mine // 4,
        "tm": 2 * lax.rem(mine, 4) + i // 4,
        "space": lax.rem(jnp.int32(i), 4) if not isinstance(i, int) else i % 4,
    }
    w_self = (w_tm == z) & (w_sp == y)
    w_home = d == mine // 4

    started = []

    def copy(a, b, n, to, m=None):
        return pltpu.make_async_remote_copy(
            src_ref=a, dst_ref=b, send_sem=send_sem.at[n], recv_sem=recv_sem.at[n if m is None else m],
            device_id=to, device_id_type=MESH,
        )

    def go(a, b, n, to, m=None):
        c = copy(a, b, n, to, m)
        c.start()
        started.append(c)
        return c

    def got(region, n):
        copy(region, region, n, {"tm": z}).wait_recv()

    barrier = pltpu.get_barrier_semaphore()

    def greet(to):
        pl.semaphore_signal(barrier, inc=1, device_id=to, device_id_type=MESH)

    pair = z + 1 - 2 * lax.rem(z, 2)
    for r in range(1, NSP):
        greet({"space": ahead(y, r, NSP)})
        greet({"tm": pair, "space": ahead(y, r, NSP)})
    greet({"tm": ahead(z, 1, NTM)})
    greet({"tm": behind(z, 1, NTM)})
    for r in range(1, NDP):
        greet({"dp": ahead(d, r, NDP)})

    p = lax.broadcasted_iota(jnp.int32, (CELLS, 4 * CELLS), 0)
    q = lax.broadcasted_iota(jnp.int32, (CELLS, 4 * CELLS), 1)
    pool = ((q >> 6) == (p >> 4)) & (((q & 31) >> 1) == (p & 15))
    pool = jnp.where(pool, 1.0, 0.0).astype(BF16)
    for f in range(2):
        pooled = jnp.dot(pool, ups_ref[f], preferred_element_type=F32)
        gz[2 * z + f, y] = pooled.astype(BF16)
    dhb[...] = jnp.zeros_like(dhb)
    dk[...] = jnp.zeros_like(dk)

    own_to = 8 * mine + d
    self_t = jnp.where(own_to == line, 1, 0)
    pl.semaphore_wait(barrier, 2 * (NSP - 1) + 2 + NDP - 1)

    def part_b(zo, yo, f=0, n=2):
        return gz.at[pl.ds(2 * zo + f, n), yo, pl.ds(LEFT, CELLS - LEFT)]

    def part_a(zo, yo, f=0, n=2):
        return gz.at[pl.ds(2 * zo + f, n), yo, pl.ds(0, LEFT)]

    zr, zl = {"tm": ahead(z, 1, NTM)}, {"tm": behind(z, 1, NTM)}
    yr, yl = {"space": ahead(y, 1, NSP)}, {"space": behind(y, 1, NSP)}
    yo_r, yo_l, yo_2 = ahead(y, 1, NSP), behind(y, 1, NSP), ahead(y, 2, NSP)

    def tm_step(region, base, h):
        frames = (dict(f=0, n=2),) * 2 if h < 4 else (dict(f=0, n=1), dict(f=1, n=1))
        for way, (to, o) in enumerate(((zr, behind(z, h - 1, NTM)), (zl, ahead(z, h - 1, NTM)))):
            a = region(o, **frames[way])
            go(a, a, base + 2 * (h - 1) + way, to)

    def tm_got(region, base, h):
        frames = (dict(f=0, n=2),) * 2 if h < 4 else (dict(f=0, n=1), dict(f=1, n=1))
        for way, o in enumerate((behind(z, h, NTM), ahead(z, h, NTM))):
            got(region(o, **frames[way]), base + 2 * (h - 1) + way)

    def sp_send(region, base, zo):
        a = region(zo, y)
        go(a, a, base, yr)
        go(a, a, base + 1, yl)

    def sp_forward(region, base, zo):
        got(region(zo, yo_l), base)
        a = region(zo, yo_l, 0, 1)
        go(a, a, base + 2, yr)
        got(region(zo, yo_r), base + 1)
        a = region(zo, yo_r, 1, 1)
        go(a, a, base + 3, yl)

    def sp_got(region, base, zo):
        got(region(zo, yo_2, 0, 1), base + 2)
        got(region(zo, yo_2, 1, 1), base + 3)

    steps = (0, -1, 1, -2, 2, -3, 3, 4)
    origin = [lax.rem(z + s + NTM, NTM) for s in steps]
    b_row = lambda zo, yo, f=0, n=2: part_b(zo, yo, f, n)
    b_tm = lambda zo, f=0, n=2: part_b(zo, y, f, n)

    sides = (y, yo_l, yo_r, yo_2)
    a_tm = [lambda zo, f=0, n=2, yo=yo: part_a(zo, yo, f, n) for yo in sides]
    near = [(0,), (1, 2), (3, 4), (5, 6), (7,)]

    def wave_b(h):
        tm_got(b_tm, B_TM, h)
        if h < 4:
            tm_step(b_tm, B_TM, h + 1)
        for b in near[h]:
            sp_send(b_row, B_SP + 4 * b, origin[b])

    def wave_a(h):
        for q in range(4):
            tm_got(a_tm[q], A_TM + 8 * q, h)
            if h < 4:
                tm_step(a_tm[q], A_TM + 8 * q, h + 1)

    def forward(h):
        for b in near[h]:
            sp_forward(b_row, B_SP + 4 * b, origin[b])

    def complete(h):
        for b in near[h]:
            sp_got(b_row, B_SP + 4 * b, origin[b])

    def block(h, i):
        return lax.rem(z + (2 * i - 1) * h + NTM, NTM)

    cell = lax.broadcasted_iota(jnp.int32, (8, GS, CELLS), 2)
    ix, iy = cell & (TW - 1), cell >> 4

    def inside(dy, dx):
        ok = None
        for cond in (
            [iy + dy >= 0] if dy < 0 else [iy + dy < TH] if dy > 0 else []
        ) + ([ix + dx >= 0] if dx < 0 else [ix + dx < TW] if dx > 0 else []):
            ok = cond if ok is None else ok & cond
        return ok

    nt = (((1,), (1,)), ((), ()))

    def dhidden(h):
        def frame(n, _):
            f = 2 * block(h, n // 2) + lax.rem(n, 2)
            v = lax.dot_general(
                wall[...], gz[f].reshape(TILES * CELLS, COUT), nt, preferred_element_type=F32
            )
            for t in range(TILES):
                lanes = slice(t * CELLS, (t + 1) * CELLS)
                rsd[TILES * f + t] = v[3 * ROWS :, lanes]
                for kt in range(3):
                    out = None
                    for s in range(9):
                        dy, dx = s // 3 - 1, s % 3 - 1
                        w = v[kt * ROWS + s * GS : kt * ROWS + (s + 1) * GS, lanes]
                        if s != 4:
                            w = pltpu.roll(w, (TW * dy + dx) % CELLS, 1)
                            w = jnp.where(inside(-dy, -dx)[0], w, 0.0)
                        out = w if out is None else out + w
                    dhb[TILES * (f + kt) + t] += out
            return 0

        lax.fori_loop(0, 2 * len(near[h]), frame, 0)

    def dweight(h):
        def one(n, _):
            i = block(h, n)
            g = gz[pl.ds(2 * i, 2)].reshape(1024, COUT)
            for kt in range(3):
                a = a9[:, pl.ds(pl.multiple_of(1024 * i + 512 * kt, 512), 1024)]
                dk[9 * kt : 9 * kt + 9] += jnp.dot(a, g, preferred_element_type=F32).reshape(9, GS, COUT)
            return 0

        lax.fori_loop(0, len(near[h]), one, 0)

    sp_send(part_a, A_SP, z)
    tm_step(b_tm, B_TM, 1)
    sp_send(b_row, B_SP, z)

    to_group = copy(w_ref, wbuf.at[w_piece], WGT + 8, {"tm": w_tm, "space": w_sp}, WGT + w_piece)

    @pl.when(jnp.logical_not(w_self))
    def _():
        to_group.start()

    @pl.when(w_self)
    def _():
        pltpu.make_async_copy(w_ref, wbuf.at[w_piece], recv_sem.at[WGT + w_piece]).start()

    wave_b(1)
    sp_forward(part_a, A_SP, z)
    for q in range(3):
        tm_step(a_tm[q], A_TM + 8 * q, 1)
    wave_b(2)

    for r in range(1, NSP):
        yo = ahead(y, r, NSP)
        go(
            lat_ref.at[:, :, :, pl.ds(pl.multiple_of(yo * 128, 128), 128)],
            ybuf.at[y], L_SP + r, {"space": yo},
        )
    own = pltpu.make_async_copy(
        lat_ref.at[:, :, :, pl.ds(pl.multiple_of(y * 128, 128), 128)], ybuf.at[y], own_sem.at[0]
    )
    own.start()

    sp_got(part_a, A_SP, z)
    tm_step(a_tm[3], A_TM + 24, 1)
    forward(0)

    @pl.when(w_home)
    def _():
        for i in range(8):
            got(wbuf.at[i], WGT + i)
        for r in range(1, NDP):
            copy(wbuf, wbuf, WGT + 9 + r, {"dp": ahead(d, r, NDP)}, WGT + 9).start()

    wave_b(3)
    wave_a(1)
    wave_b(4)

    own.wait()
    for r in range(1, NSP):
        got(ybuf.at[behind(y, r, NSP)], L_SP + r)
    owners = [owner_ref[t] for t in range(TILES)]
    ranks = [
        jnp.minimum(
            sum([(owners[u] == owners[t]).astype(jnp.int32) for u in range(t)], jnp.int32(0)), CAP - 1
        )
        for t in range(TILES)
    ]
    for t in range(TILES):
        for f in range(2):
            v = ybuf[owners[t], f, ranks[t]].astype(F32)
            zsend[:, f * TILES + t] = v.T.reshape(NTM, GS, CELLS).astype(BF16)
    for r in range(1, NTM):
        zo = ahead(z, r, NTM)
        go(zsend.at[place(zo)], xbuf.at[z], L_TM + r, {"tm": zo})
    xbuf[z] = zsend[tz]

    @pl.when(jnp.logical_not(w_home))
    def _():
        got(wbuf, WGT + 9)

    for i in range(8):
        wf[:, 2 * i : 2 * i + 2, :] = wbuf[i].astype(F32)
    wall[0 : 3 * ROWS, :] = wf[...].reshape(3 * ROWS, COUT).astype(BF16)
    pick_r = lax.broadcasted_iota(jnp.int32, (GS, COUT), 0)
    pick_o = lax.broadcasted_iota(jnp.int32, (GS, COUT), 1)
    wall[3 * ROWS : 3 * ROWS + GS, :] = jnp.where(pick_o == mine * GS + pick_r, 1.0, 0.0).astype(BF16)

    forward(1)
    complete(0)
    dhidden(0)
    wave_a(2)
    forward(2)
    complete(1)
    dhidden(1)

    for r in range(1, NTM):
        got(xbuf.at[behind(z, r, NTM)], L_TM + r)
    count = float(FR * TILES * CELLS * GS)
    zero = jnp.zeros((GS, CELLS), F32)

    def whole(v):
        return jnp.sum(jnp.sum(v, axis=1, keepdims=True), axis=0, keepdims=True)

    def total(i, acc):
        return acc + jnp.sum(xbuf[i].astype(F32), axis=0)

    mean = whole(lax.fori_loop(0, NTM, total, zero)) / count

    def spread(i, acc):
        v = xbuf[i].astype(F32) - mean
        return acc + jnp.sum(v * v, axis=0)

    inverse = lax.rsqrt(whole(lax.fori_loop(0, NTM, spread, zero)) / count + EPS)

    row16 = lax.broadcasted_iota(jnp.int32, (GS, CELLS), 0)
    lane16 = lax.broadcasted_iota(jnp.int32, (GS, CELLS), 1)
    diag = lane16 == tz * GS + row16

    def column(ref):
        return jnp.sum(jnp.where(diag, ref[pl.ds(y, 1), :], 0.0), axis=1, keepdims=True)

    gamma, beta = column(gamma_ref), column(beta_ref)

    def taps(i, _):
        normed = (xbuf[i].astype(F32) - mean) * inverse
        act = normed * gamma + beta
        sig = jax.nn.sigmoid(act)
        xh[i] = normed
        ds[i] = sig * (1.0 + act * (1.0 - sig))
        hidden = (act * sig).astype(BF16).astype(F32)
        base = pl.multiple_of((i + 1) * 1024, 1024)
        for s in range(9):
            dy, dx = s // 3 - 1, s % 3 - 1
            v = hidden
            if s != 4:
                v = pltpu.roll(v, (-(TW * dy + dx)) % CELLS, 2)
                v = jnp.where(inside(dy, dx), v, 0.0)
            v = v.astype(BF16)
            for j in range(8):
                a9[s * GS : (s + 1) * GS, pl.ds(base + j * CELLS, CELLS)] = v[j]
        return 0

    lax.fori_loop(0, NTM, taps, 0)
    a9[:, 0:512] = a9[:, 1024:1536]
    a9[:, 512:1024] = a9[:, 1024:1536]

    wave_a(3)
    forward(3)
    dweight(0)
    dweight(1)
    complete(2)
    dhidden(2)
    dweight(2)
    forward(4)
    complete(3)
    dhidden(3)
    dweight(3)
    wave_a(4)
    complete(4)
    dweight(4)

    rscale = 1.0 / math.sqrt(NDP * FR * TILES * CELLS)
    for i in range(8):
        dsend[i] = dk[:, 2 * i : 2 * i + 2, :] * rscale
    for r in range(1, NDP):
        to = ahead(d, r, NDP)
        go(dsend.at[to], drecv.at[d], D_DP + r, {"dp": to})
    drecv[d] = dsend[d]

    dhidden(4)
    dhb[8:12] = dhb[8:12] + (dhb[0:4] + dhb[4:8])

    def gains(i, acc):
        dact = dhb[pl.ds(8 + 8 * i, 8)] * ds[i]
        dhb[pl.ds(8 + 8 * i, 8)] = dact
        return acc[0] + jnp.sum(dact * xh[i], axis=0), acc[1] + jnp.sum(dact, axis=0)

    dgam, dbet = lax.fori_loop(0, NTM, gains, (zero, zero))
    dgam = jnp.sum(dgam, axis=1, keepdims=True)
    dbet = jnp.sum(dbet, axis=1, keepdims=True)
    m1 = jnp.sum(dbet * gamma, axis=0, keepdims=True) / count
    m2 = jnp.sum(dgam * gamma, axis=0, keepdims=True) / count

    def dinput(i, _):
        v = inverse * (dhb[pl.ds(8 + 8 * i, 8)] * gamma - m1 - xh[i] * m2)
        dxs[i] = (v + rsd[pl.ds(8 * i, 8)]).astype(BF16)
        return 0

    lax.fori_loop(0, NTM, dinput, 0)

    def of_frame(ref, i, f):
        return ref.at[i, pl.ds(f * TILES, TILES)]

    for f in range(2):
        for r in range(1, NTM):
            zo = ahead(z, r, NTM)
            go(of_frame(dxs, zo, f), of_frame(zback, tz, f), D_TM + 8 * f + r, {"tm": zo})
    zback[tz] = dxs[z]

    gown[0:1, :] = jnp.sum(jnp.where(diag, dgam * rscale, 0.0), axis=0, keepdims=True)
    gown[1:2, :] = jnp.sum(jnp.where(diag, dbet * rscale, 0.0), axis=0, keepdims=True)
    for r in range(1, NDP):
        to = ahead(d, r, NDP)
        go(gown, gdp.at[d], G_DP + r, {"dp": to})
    gdp[d] = gown[...]

    lanes = pl.ds(pl.multiple_of(y * 128, 128), 128)

    def to_slots(f):
        for r in range(1, NTM):
            got(of_frame(zback, place(behind(z, r, NTM)), f), D_TM + 8 * f + r)
        for t in range(TILES):
            v = zback[:, f * TILES + t].astype(F32).reshape(NTM * GS, CELLS)
            tback[f, t] = v.T.astype(BF16)
        for yo in range(NSP):
            for j in range(CAP):
                tile, live = jnp.int32(0), jnp.int32(0)
                for t in range(TILES):
                    here = (owners[t] == yo) & (ranks[t] == j)
                    tile, live = jnp.where(here, t, tile), jnp.where(here, 1, live)
                v = tback[f, tile]
                ysend[f, yo, j] = jnp.where(live > 0, v, jnp.zeros_like(v))
        for r in range(1, NSP):
            yo = ahead(y, r, NSP)
            go(ysend.at[f, yo], dlat_ref.at[f, :, :, lanes], D_SP + 4 * f + r, {"space": yo})
        own = pltpu.make_async_copy(ysend.at[f, y], dlat_ref.at[f, :, :, lanes], own_sem.at[1 + f])
        own.start()
        return own

    owns = [to_slots(0)]

    for r in range(1, NDP):
        got(gdp.at[behind(d, r, NDP)], G_DP + r)
    acc = gdp[0]
    for i in range(1, NDP):
        acc = acc + gdp[i]
    gsum[...] = acc
    for r in range(NTM):
        for q in range(NSP):
            if r or q:
                to = {"tm": ahead(z, r, NTM), "space": ahead(y, q, NSP)}
                go(gsum, gall.at[z, y], G_ALL + r * NSP + q, to)
    gall[z, y] = gsum[...]

    owns.append(to_slots(1))

    for r in range(1, NDP):
        got(drecv.at[behind(d, r, NDP)], D_DP + r)
    acc = drecv[0]
    for i in range(1, NDP):
        acc = acc + drecv[i]
    dsum[...] = acc
    to_owner = copy(dsum, dw_ref, D_OWN, src(d))

    @pl.when(self_t == 0)
    def _():
        to_owner.start()

    @pl.when(self_t == 1)
    def _():
        pltpu.make_async_copy(dsum, dw_ref, recv_sem.at[D_OWN]).start()

    for r in range(NTM):
        for q in range(NSP):
            if r or q:
                got(gall.at[behind(z, r, NTM), behind(y, q, NSP)], G_ALL + r * NSP + q)
    for s in range(NSP):
        acc = gall[0, s]
        for i in range(1, NTM):
            acc = acc + gall[i, s]
        dgam_ref[s : s + 1, :] = acc[0:1]
        dbet_ref[s : s + 1, :] = acc[1:2]

    for f in range(2):
        owns[f].wait()
        for r in range(1, NSP):
            yo = behind(y, r, NSP)
            got(dlat_ref.at[f, :, :, pl.ds(pl.multiple_of(yo * 128, 128), 128)], D_SP + 4 * f + r)
    got(dw_ref, D_OWN)
    for c in started:
        c.wait_send()

    @pl.when(self_t == 0)
    def _():
        copy(dsum, dw_ref, D_OWN, src(d)).wait_send()

    @pl.when(jnp.logical_not(w_self))
    def _():
        copy(w_ref, wbuf.at[w_piece], WGT + 8, {"tm": z}).wait_send()

    @pl.when(w_home)
    def _():
        for r in range(1, NDP):
            copy(wbuf, wbuf, WGT + 9 + r, {"dp": ahead(d, r, NDP)}, WGT + 9).wait_send()


def written(*refs):
    for a, b in zip(refs[:4], refs[4:]):
        b[...] = a[...]


def shards(latents, owner, gamma, beta, weight, upstream):
    vmem = pl.BlockSpec(memory_space=pltpu.VMEM)
    hbm = pl.BlockSpec(memory_space=pl.ANY)
    scratch = [
        ((FR, TILES, CELLS, COUT), BF16),
        ((NSP, 2, CAP, CELLS, 128), BF16),
        ((NTM, 8, GS, CELLS), BF16),
        ((NTM, 8, GS, CELLS), BF16),
        ((8, TAPS, 2, COUT), BF16),
        ((TAPS, GS, COUT), F32),
        ((3 * ROWS + GS, COUT), BF16),
        ((ROWS, 512 * (FR + 2)), BF16),
        ((NTM, 8, GS, CELLS), F32),
        ((NTM, 8, GS, CELLS), F32),
        ((TILES * (FR + 2), GS, CELLS), F32),
        ((TILES * FR, GS, CELLS), F32),
        ((TAPS, GS, COUT), F32),
        ((8, TAPS, 2, COUT), F32),
        ((8, TAPS, 2, COUT), F32),
        ((TAPS, 2, COUT), F32),
        ((NTM, 8, GS, CELLS), BF16),
        ((NTM, 8, GS, CELLS), BF16),
        ((2, TILES, CELLS, 128), BF16),
        ((2, NSP, CAP, CELLS, 128), BF16),
        ((2, 128), F32),
        ((NDP, 2, 128), F32),
        ((2, 128), F32),
        ((NTM, NSP, 2, 128), F32),
    ]
    dlat, dw, dgam, dbet = pl.pallas_call(
        body,
        out_shape=(
            jax.ShapeDtypeStruct((2, CAP, CELLS, C), BF16),
            jax.ShapeDtypeStruct((TAPS, 2, COUT), F32),
            jax.ShapeDtypeStruct((4, 128), F32),
            jax.ShapeDtypeStruct((4, 128), F32),
        ),
        in_specs=[pl.BlockSpec(memory_space=pltpu.SMEM), vmem, vmem, vmem, vmem, vmem],
        out_specs=(hbm, hbm, vmem, vmem),
        scratch_shapes=[pltpu.VMEM(s, t) for s, t in scratch]
        + [
            pltpu.SemaphoreType.DMA((N_SEM,)),
            pltpu.SemaphoreType.DMA((N_SEM,)),
            pltpu.SemaphoreType.DMA((3,)),
        ],
        compiler_params=pltpu.CompilerParams(
            collective_id=0, has_side_effects=True, vmem_limit_bytes=56 * 2**20
        ),
    )(
        owner.reshape(TILES),
        gamma.reshape(4, 128),
        beta.reshape(4, 128),
        latents[0],
        upstream.reshape(2, 4 * CELLS, COUT),
        weight.transpose(1, 0, 2),
    )
    dlat, dw, dgam, dbet = pl.pallas_call(
        written,
        out_shape=[jax.ShapeDtypeStruct(v.shape, v.dtype) for v in (dlat, dw, dgam, dbet)],
        in_specs=[vmem] * 4,
        out_specs=[vmem] * 4,
    )(dlat, dw, dgam, dbet)
    return dlat[None], dw.transpose(1, 0, 2), dgam.reshape(C), dbet.reshape(C)


def solution(mesh):
    return jax.shard_map(
        shards,
        mesh=mesh,
        in_specs=(
            P("dp", "tm", "space", None, None),
            P("dp", None, None),
            P(),
            P(),
            P(("dp", "tm", "space"), None, None),
            P("dp", "tm", "space", None, None),
        ),
        out_specs=(
            P("dp", "tm", "space", None, None),
            P(("dp", "tm", "space"), None, None),
            P(),
            P(),
        ),
        check_vma=False,
    )
```

```python
import math

import jax
import jax.numpy as jnp
from jax import lax
from jax.experimental import pallas as pl
from jax.experimental.pallas import tpu as pltpu
from jax.sharding import PartitionSpec as P

MESH = pl.DeviceIdType.MESH
F32 = jnp.float32
BF16 = jnp.bfloat16
EPS = 1e-06

NDP, NTM, NSP = 8, 8, 4
GROUPS = 32
GS = 16
FR = 16
TILES = 4
CAP = 2
TH, TW = 8, 16
CELLS = TH * TW
C, COUT = 512, 256
TAPS = 27
ROWS = 9 * GS
LEFT = 48

B_TM, B_SP, A_SP, A_TM = 0, 8, 40, 44
L_SP, L_TM, WGT = 76, 80, 88
D_TM, D_DP, G_DP, D_SP, D_OWN, G_ALL = 112, 120, 136, 144, 176, 178
N_SEM = 210
HALVES = ((0, 14), (14, TAPS - 14))


def body(
    owner_ref, gamma_ref, beta_ref, lat_ref, ups_ref, w_ref,
    slab_ref, dw_ref, dgam_ref, dbet_ref,
    gz, ybuf, zsend, xbuf, wbuf, wf, wall, a9, xh, ds, dhb, rsd, dk, dsend, drecv, dsum,
    dxs, zback, ysend, gown, gdp, gsum, gall, send_sem, recv_sem, own_sem,
):
    d, z, y = lax.axis_index("dp"), lax.axis_index("tm"), lax.axis_index("space")
    ahead = lambda v, r, n: lax.rem(v + r, n)
    behind = lambda v, r, n: lax.rem(v - r + n, n)
    line = (d * NTM + z) * NSP + y
    place = lambda v: 4 * lax.rem(v, 2) + v // 2
    tz = place(z)
    mine = y * NTM + tz
    w_group = line // 8
    w_tm, w_sp = 2 * lax.rem(w_group, 4) + lax.rem(w_group, NTM) // 4, w_group // NTM
    w_piece = lax.rem(line, 8)
    src = lambda i: {
        "dp": mine // 4,
        "tm": 2 * lax.rem(mine, 4) + i // 4,
        "space": lax.rem(jnp.int32(i), 4) if not isinstance(i, int) else i % 4,
    }
    w_self = (w_tm == z) & (w_sp == y)
    w_home = d == mine // 4

    started = []

    def copy(a, b, n, to, m=None):
        return pltpu.make_async_remote_copy(
            src_ref=a, dst_ref=b, send_sem=send_sem.at[n], recv_sem=recv_sem.at[n if m is None else m],
            device_id=to, device_id_type=MESH,
        )

    def go(a, b, n, to, m=None):
        c = copy(a, b, n, to, m)
        c.start()
        started.append(c)
        return c

    def got(region, n):
        copy(region, region, n, {"tm": z}).wait_recv()

    barrier = pltpu.get_barrier_semaphore()

    def greet(to):
        pl.semaphore_signal(barrier, inc=1, device_id=to, device_id_type=MESH)

    pair = z + 1 - 2 * lax.rem(z, 2)
    for r in range(1, NSP):
        greet({"space": ahead(y, r, NSP)})
        greet({"tm": pair, "space": ahead(y, r, NSP)})
    greet({"tm": ahead(z, 1, NTM)})
    greet({"tm": behind(z, 1, NTM)})
    for r in range(1, NDP):
        greet({"dp": ahead(d, r, NDP)})

    p = lax.broadcasted_iota(jnp.int32, (CELLS, 4 * CELLS), 0)
    q = lax.broadcasted_iota(jnp.int32, (CELLS, 4 * CELLS), 1)
    pool = ((q >> 6) == (p >> 4)) & (((q & 31) >> 1) == (p & 15))
    pool = jnp.where(pool, 1.0, 0.0).astype(BF16)
    for f in range(2):
        pooled = jnp.dot(pool, ups_ref[f], preferred_element_type=F32)
        gz[2 * z + f, y] = pooled.astype(BF16)
    dhb[...] = jnp.zeros_like(dhb)
    dk[...] = jnp.zeros_like(dk)

    own_to = 8 * mine + d
    self_t = jnp.where(own_to == line, 1, 0)
    pl.semaphore_wait(barrier, 2 * (NSP - 1) + 2 + NDP - 1)

    def part_b(zo, yo, f=0, n=2):
        return gz.at[pl.ds(2 * zo + f, n), yo, pl.ds(LEFT, CELLS - LEFT)]

    def part_a(zo, yo, f=0, n=2):
        return gz.at[pl.ds(2 * zo + f, n), yo, pl.ds(0, LEFT)]

    zr, zl = {"tm": ahead(z, 1, NTM)}, {"tm": behind(z, 1, NTM)}
    yr, yl = {"space": ahead(y, 1, NSP)}, {"space": behind(y, 1, NSP)}
    yo_r, yo_l, yo_2 = ahead(y, 1, NSP), behind(y, 1, NSP), ahead(y, 2, NSP)

    def tm_step(region, base, h):
        frames = (dict(f=0, n=2),) * 2 if h < 4 else (dict(f=0, n=1), dict(f=1, n=1))
        for way, (to, o) in enumerate(((zr, behind(z, h - 1, NTM)), (zl, ahead(z, h - 1, NTM)))):
            a = region(o, **frames[way])
            go(a, a, base + 2 * (h - 1) + way, to)

    def tm_got(region, base, h):
        frames = (dict(f=0, n=2),) * 2 if h < 4 else (dict(f=0, n=1), dict(f=1, n=1))
        for way, o in enumerate((behind(z, h, NTM), ahead(z, h, NTM))):
            got(region(o, **frames[way]), base + 2 * (h - 1) + way)

    def sp_send(region, base, zo):
        a = region(zo, y)
        go(a, a, base, yr)
        go(a, a, base + 1, yl)

    def sp_forward(region, base, zo):
        got(region(zo, yo_l), base)
        a = region(zo, yo_l, 0, 1)
        go(a, a, base + 2, yr)
        got(region(zo, yo_r), base + 1)
        a = region(zo, yo_r, 1, 1)
        go(a, a, base + 3, yl)

    def sp_got(region, base, zo):
        got(region(zo, yo_2, 0, 1), base + 2)
        got(region(zo, yo_2, 1, 1), base + 3)

    steps = (0, -1, 1, -2, 2, -3, 3, 4)
    origin = [lax.rem(z + s + NTM, NTM) for s in steps]
    b_row = lambda zo, yo, f=0, n=2: part_b(zo, yo, f, n)
    b_tm = lambda zo, f=0, n=2: part_b(zo, y, f, n)

    sides = (y, yo_l, yo_r, yo_2)
    a_tm = [lambda zo, f=0, n=2, yo=yo: part_a(zo, yo, f, n) for yo in sides]
    near = [(0,), (1, 2), (3, 4), (5, 6), (7,)]

    def wave_b(h):
        tm_got(b_tm, B_TM, h)
        if h < 4:
            tm_step(b_tm, B_TM, h + 1)
        for b in near[h]:
            sp_send(b_row, B_SP + 4 * b, origin[b])

    def wave_a(h):
        for q in range(4):
            tm_got(a_tm[q], A_TM + 8 * q, h)
            if h < 4:
                tm_step(a_tm[q], A_TM + 8 * q, h + 1)

    def forward(h):
        for b in near[h]:
            sp_forward(b_row, B_SP + 4 * b, origin[b])

    def complete(h):
        for b in near[h]:
            sp_got(b_row, B_SP + 4 * b, origin[b])

    def block(h, i):
        return lax.rem(z + (2 * i - 1) * h + NTM, NTM)

    cell = lax.broadcasted_iota(jnp.int32, (8, GS, CELLS), 2)
    ix, iy = cell & (TW - 1), cell >> 4

    def inside(dy, dx):
        ok = None
        for cond in (
            [iy + dy >= 0] if dy < 0 else [iy + dy < TH] if dy > 0 else []
        ) + ([ix + dx >= 0] if dx < 0 else [ix + dx < TW] if dx > 0 else []):
            ok = cond if ok is None else ok & cond
        return ok

    nt = (((1,), (1,)), ((), ()))

    def dhidden(h):
        def frame(n, _):
            f = 2 * block(h, n // 2) + lax.rem(n, 2)
            v = lax.dot_general(
                wall[...], gz[f].reshape(TILES * CELLS, COUT), nt, preferred_element_type=F32
            )
            for t in range(TILES):
                lanes = slice(t * CELLS, (t + 1) * CELLS)
                rsd[TILES * f + t] = v[3 * ROWS :, lanes]
                for kt in range(3):
                    out = None
                    for s in range(9):
                        dy, dx = s // 3 - 1, s % 3 - 1
                        w = v[kt * ROWS + s * GS : kt * ROWS + (s + 1) * GS, lanes]
                        if s != 4:
                            w = pltpu.roll(w, (TW * dy + dx) % CELLS, 1)
                            w = jnp.where(inside(-dy, -dx)[0], w, 0.0)
                        out = w if out is None else out + w
                    dhb[TILES * (f + kt) + t] += out
            return 0

        lax.fori_loop(0, 2 * len(near[h]), frame, 0)

    def dweight(h):
        def one(n, _):
            i = block(h, n)
            g = gz[pl.ds(2 * i, 2)].reshape(1024, COUT)
            for kt in range(3):
                a = a9[:, pl.ds(pl.multiple_of(1024 * i + 512 * kt, 512), 1024)]
                dk[9 * kt : 9 * kt + 9] += jnp.dot(a, g, preferred_element_type=F32).reshape(9, GS, COUT)
            return 0

        lax.fori_loop(0, len(near[h]), one, 0)

    sp_send(part_a, A_SP, z)
    tm_step(b_tm, B_TM, 1)
    sp_send(b_row, B_SP, z)

    to_group = copy(w_ref, wbuf.at[w_piece], WGT + 8, {"tm": w_tm, "space": w_sp}, WGT + w_piece)

    @pl.when(jnp.logical_not(w_self))
    def _():
        to_group.start()

    @pl.when(w_self)
    def _():
        pltpu.make_async_copy(w_ref, wbuf.at[w_piece], recv_sem.at[WGT + w_piece]).start()

    wave_b(1)
    sp_forward(part_a, A_SP, z)
    for q in range(3):
        tm_step(a_tm[q], A_TM + 8 * q, 1)
    wave_b(2)

    for r in range(1, NSP):
        yo = ahead(y, r, NSP)
        go(
            lat_ref.at[:, :, :, pl.ds(pl.multiple_of(yo * 128, 128), 128)],
            ybuf.at[y], L_SP + r, {"space": yo},
        )
    own = pltpu.make_async_copy(
        lat_ref.at[:, :, :, pl.ds(pl.multiple_of(y * 128, 128), 128)], ybuf.at[y], own_sem.at[0]
    )
    own.start()

    sp_got(part_a, A_SP, z)
    tm_step(a_tm[3], A_TM + 24, 1)
    forward(0)

    @pl.when(w_home)
    def _():
        for i in range(8):
            got(wbuf.at[i], WGT + i)
        for r in range(1, NDP):
            copy(wbuf, wbuf, WGT + 9 + r, {"dp": ahead(d, r, NDP)}, WGT + 9).start()

    wave_b(3)
    wave_a(1)
    wave_b(4)

    own.wait()
    for r in range(1, NSP):
        got(ybuf.at[behind(y, r, NSP)], L_SP + r)
    owners = [owner_ref[t] for t in range(TILES)]
    ranks = [
        jnp.minimum(
            sum([(owners[u] == owners[t]).astype(jnp.int32) for u in range(t)], jnp.int32(0)), CAP - 1
        )
        for t in range(TILES)
    ]
    for t in range(TILES):
        for f in range(2):
            v = ybuf[owners[t], f, ranks[t]].astype(F32)
            zsend[:, f * TILES + t] = v.T.reshape(NTM, GS, CELLS).astype(BF16)
    for r in range(1, NTM):
        zo = ahead(z, r, NTM)
        go(zsend.at[place(zo)], xbuf.at[z], L_TM + r, {"tm": zo})
    xbuf[z] = zsend[tz]

    @pl.when(jnp.logical_not(w_home))
    def _():
        got(wbuf, WGT + 9)

    for i in range(8):
        wf[:, 2 * i : 2 * i + 2, :] = wbuf[i].astype(F32)
    wall[0 : 3 * ROWS, :] = wf[...].reshape(3 * ROWS, COUT).astype(BF16)
    pick_r = lax.broadcasted_iota(jnp.int32, (GS, COUT), 0)
    pick_o = lax.broadcasted_iota(jnp.int32, (GS, COUT), 1)
    wall[3 * ROWS : 3 * ROWS + GS, :] = jnp.where(pick_o == mine * GS + pick_r, 1.0, 0.0).astype(BF16)

    forward(1)
    complete(0)
    dhidden(0)
    wave_a(2)
    forward(2)
    complete(1)
    dhidden(1)

    for r in range(1, NTM):
        got(xbuf.at[behind(z, r, NTM)], L_TM + r)
    count = float(FR * TILES * CELLS * GS)
    zero = jnp.zeros((GS, CELLS), F32)

    def whole(v):
        return jnp.sum(jnp.sum(v, axis=1, keepdims=True), axis=0, keepdims=True)

    def total(i, acc):
        return acc + jnp.sum(xbuf[i].astype(F32), axis=0)

    mean = whole(lax.fori_loop(0, NTM, total, zero)) / count

    def spread(i, acc):
        v = xbuf[i].astype(F32) - mean
        return acc + jnp.sum(v * v, axis=0)

    inverse = lax.rsqrt(whole(lax.fori_loop(0, NTM, spread, zero)) / count + EPS)

    row16 = lax.broadcasted_iota(jnp.int32, (GS, CELLS), 0)
    lane16 = lax.broadcasted_iota(jnp.int32, (GS, CELLS), 1)
    diag = lane16 == tz * GS + row16

    def column(ref):
        return jnp.sum(jnp.where(diag, ref[pl.ds(y, 1), :], 0.0), axis=1, keepdims=True)

    gamma, beta = column(gamma_ref), column(beta_ref)

    def taps(i, _):
        normed = (xbuf[i].astype(F32) - mean) * inverse
        act = normed * gamma + beta
        sig = jax.nn.sigmoid(act)
        xh[i] = normed
        ds[i] = sig * (1.0 + act * (1.0 - sig))
        hidden = (act * sig).astype(BF16).astype(F32)
        base = pl.multiple_of((i + 1) * 1024, 1024)
        for s in range(9):
            dy, dx = s // 3 - 1, s % 3 - 1
            v = hidden
            if s != 4:
                v = pltpu.roll(v, (-(TW * dy + dx)) % CELLS, 2)
                v = jnp.where(inside(dy, dx), v, 0.0)
            v = v.astype(BF16)
            for j in range(8):
                a9[s * GS : (s + 1) * GS, pl.ds(base + j * CELLS, CELLS)] = v[j]
        return 0

    lax.fori_loop(0, NTM, taps, 0)
    a9[:, 0:512] = a9[:, 1024:1536]
    a9[:, 512:1024] = a9[:, 1024:1536]

    wave_a(3)
    forward(3)
    dweight(0)
    dweight(1)
    complete(2)
    dhidden(2)
    dweight(2)
    forward(4)
    complete(3)
    dhidden(3)
    dweight(3)
    wave_a(4)
    complete(4)
    dweight(4)

    rscale = 1.0 / math.sqrt(NDP * FR * TILES * CELLS)
    for i in range(8):
        dsend[i] = dk[:, 2 * i : 2 * i + 2, :] * rscale
    for h, (k0, kn) in enumerate(HALVES):
        for r in range(1, NDP):
            to = ahead(d, r, NDP)
            go(
                dsend.at[to, pl.ds(k0, kn)], drecv.at[d, pl.ds(k0, kn)], D_DP + 8 * h + r, {"dp": to}
            )
    drecv[d] = dsend[d]

    dhidden(4)
    dhb[8:12] = dhb[8:12] + (dhb[0:4] + dhb[4:8])

    def gains(i, acc):
        dact = dhb[pl.ds(8 + 8 * i, 8)] * ds[i]
        dhb[pl.ds(8 + 8 * i, 8)] = dact
        return acc[0] + jnp.sum(dact * xh[i], axis=0), acc[1] + jnp.sum(dact, axis=0)

    dgam, dbet = lax.fori_loop(0, NTM, gains, (zero, zero))
    dgam = jnp.sum(dgam, axis=1, keepdims=True)
    dbet = jnp.sum(dbet, axis=1, keepdims=True)
    m1 = jnp.sum(dbet * gamma, axis=0, keepdims=True) / count
    m2 = jnp.sum(dgam * gamma, axis=0, keepdims=True) / count

    def dinput(i, _):
        v = inverse * (dhb[pl.ds(8 + 8 * i, 8)] * gamma - m1 - xh[i] * m2)
        dxs[i] = (v + rsd[pl.ds(8 * i, 8)]).astype(BF16)
        return 0

    lax.fori_loop(0, NTM, dinput, 0)

    for r in range(1, NTM):
        zo = ahead(z, r, NTM)
        go(dxs.at[zo], zback.at[tz], D_TM + r, {"tm": zo})
    zback[tz] = dxs[z]

    gown[0:1, :] = jnp.sum(jnp.where(diag, dgam * rscale, 0.0), axis=0, keepdims=True)
    gown[1:2, :] = jnp.sum(jnp.where(diag, dbet * rscale, 0.0), axis=0, keepdims=True)
    for r in range(1, NDP):
        to = ahead(d, r, NDP)
        go(gown, gdp.at[d], G_DP + r, {"dp": to})
    gdp[d] = gown[...]

    held = []
    for yo in range(NSP):
        for j in range(CAP):
            held.append([(owners[t] == yo) & (ranks[t] == j) for t in range(TILES)])
    nearest = (0, 1, 7, 2, 6, 3, 5, 4)

    def to_slots(k):
        r = nearest[k]
        p = place(behind(z, r, NTM))
        if r:
            got(zback.at[p], D_TM + r)
        tiles = [zback[p, i] for i in range(2 * TILES)]
        for yo in range(NSP):
            for j in range(CAP):
                for f in range(2):
                    v = jnp.zeros((GS, CELLS), BF16)
                    for t in range(TILES):
                        v = jnp.where(held[CAP * yo + j][t], tiles[f * TILES + t], v)
                    ysend[p, yo, f, j] = v
        for r in range(1, NSP):
            yo = ahead(y, r, NSP)
            go(ysend.at[p, yo], slab_ref.at[y, p], D_SP + 4 * k + r, {"space": yo})

    for k in range(3):
        to_slots(k)

    for r in range(1, NDP):
        got(gdp.at[behind(d, r, NDP)], G_DP + r)
    acc = gdp[0]
    for i in range(1, NDP):
        acc = acc + gdp[i]
    gsum[...] = acc
    for r in range(NTM):
        for q in range(NSP):
            if r or q:
                to = {"tm": ahead(z, r, NTM), "space": ahead(y, q, NSP)}
                go(gsum, gall.at[z, y], G_ALL + r * NSP + q, to)
    gall[z, y] = gsum[...]

    for k in range(3, NTM):
        to_slots(k)
    own = pltpu.make_async_copy(ysend.at[:, y], slab_ref.at[y], own_sem.at[1])
    own.start()

    for h, (k0, kn) in enumerate(HALVES):
        half = pl.ds(k0, kn)
        for r in range(1, NDP):
            got(drecv.at[behind(d, r, NDP), half], D_DP + 8 * h + r)
        acc = drecv[0, k0 : k0 + kn]
        for i in range(1, NDP):
            acc = acc + drecv[i, k0 : k0 + kn]
        dsum[k0 : k0 + kn] = acc
        to_owner = copy(dsum.at[half], dw_ref.at[half], D_OWN + h, src(d))

        @pl.when(self_t == 0)
        def _():
            to_owner.start()

        @pl.when(self_t == 1)
        def _():
            pltpu.make_async_copy(dsum.at[half], dw_ref.at[half], recv_sem.at[D_OWN + h]).start()

    for r in range(NTM):
        for q in range(NSP):
            if r or q:
                got(gall.at[behind(z, r, NTM), behind(y, q, NSP)], G_ALL + r * NSP + q)
    for s in range(NSP):
        acc = gall[0, s]
        for i in range(1, NTM):
            acc = acc + gall[i, s]
        dgam_ref[s : s + 1, :] = acc[0:1]
        dbet_ref[s : s + 1, :] = acc[1:2]

    own.wait()
    for k in range(NTM):
        p = place(behind(z, nearest[k], NTM))
        for r in range(1, NSP):
            got(slab_ref.at[behind(y, r, NSP), p], D_SP + 4 * k + r)
    for h, (k0, kn) in enumerate(HALVES):
        got(dw_ref.at[pl.ds(k0, kn)], D_OWN + h)
    for c in started:
        c.wait_send()

    @pl.when(self_t == 0)
    def _():
        for h, (k0, kn) in enumerate(HALVES):
            half = pl.ds(k0, kn)
            copy(dsum.at[half], dw_ref.at[half], D_OWN + h, src(d)).wait_send()

    @pl.when(jnp.logical_not(w_self))
    def _():
        copy(w_ref, wbuf.at[w_piece], WGT + 8, {"tm": z}).wait_send()

    @pl.when(w_home)
    def _():
        for r in range(1, NDP):
            copy(wbuf, wbuf, WGT + 9 + r, {"dp": ahead(d, r, NDP)}, WGT + 9).wait_send()


def written(slab_ref, *refs):
    for f in range(2):
        for j in range(CAP):
            for q in range(NSP):
                v = slab_ref[q, :, f, j].astype(F32).reshape(128, CELLS)
                refs[3][f, j, :, 128 * q : 128 * (q + 1)] = v.T.astype(BF16)
    for a, b in zip(refs[:3], refs[4:]):
        b[...] = a[...]


def shards(latents, owner, gamma, beta, weight, upstream):
    vmem = pl.BlockSpec(memory_space=pltpu.VMEM)
    hbm = pl.BlockSpec(memory_space=pl.ANY)
    scratch = [
        ((FR, TILES, CELLS, COUT), BF16),
        ((NSP, 2, CAP, CELLS, 128), BF16),
        ((NTM, 8, GS, CELLS), BF16),
        ((NTM, 8, GS, CELLS), BF16),
        ((8, TAPS, 2, COUT), BF16),
        ((TAPS, GS, COUT), F32),
        ((3 * ROWS + GS, COUT), BF16),
        ((ROWS, 512 * (FR + 2)), BF16),
        ((NTM, 8, GS, CELLS), F32),
        ((NTM, 8, GS, CELLS), F32),
        ((TILES * (FR + 2), GS, CELLS), F32),
        ((TILES * FR, GS, CELLS), F32),
        ((TAPS, GS, COUT), F32),
        ((8, TAPS, 2, COUT), F32),
        ((8, TAPS, 2, COUT), F32),
        ((TAPS, 2, COUT), F32),
        ((NTM, 8, GS, CELLS), BF16),
        ((NTM, 8, GS, CELLS), BF16),
        ((NTM, NSP, 2, CAP, GS, CELLS), BF16),
        ((2, 128), F32),
        ((NDP, 2, 128), F32),
        ((2, 128), F32),
        ((NTM, NSP, 2, 128), F32),
    ]
    slab, dw, dgam, dbet = pl.pallas_call(
        body,
        out_shape=(
            jax.ShapeDtypeStruct((NSP, NTM, 2, CAP, GS, CELLS), BF16),
            jax.ShapeDtypeStruct((TAPS, 2, COUT), F32),
            jax.ShapeDtypeStruct((4, 128), F32),
            jax.ShapeDtypeStruct((4, 128), F32),
        ),
        in_specs=[pl.BlockSpec(memory_space=pltpu.SMEM), vmem, vmem, vmem, vmem, vmem],
        out_specs=(hbm, hbm, vmem, vmem),
        scratch_shapes=[pltpu.VMEM(s, t) for s, t in scratch]
        + [
            pltpu.SemaphoreType.DMA((N_SEM,)),
            pltpu.SemaphoreType.DMA((N_SEM,)),
            pltpu.SemaphoreType.DMA((3,)),
        ],
        compiler_params=pltpu.CompilerParams(
            collective_id=0, has_side_effects=True, vmem_limit_bytes=56 * 2**20
        ),
    )(
        owner.reshape(TILES),
        gamma.reshape(4, 128),
        beta.reshape(4, 128),
        latents[0],
        upstream.reshape(2, 4 * CELLS, COUT),
        weight.transpose(1, 0, 2),
    )
    dlat, dw, dgam, dbet = pl.pallas_call(
        written,
        out_shape=[jax.ShapeDtypeStruct((2, CAP, CELLS, C), BF16)]
        + [jax.ShapeDtypeStruct(v.shape, v.dtype) for v in (dw, dgam, dbet)],
        in_specs=[vmem] * 4,
        out_specs=[vmem] * 4,
    )(slab, dw, dgam, dbet)
    return dlat[None], dw.transpose(1, 0, 2), dgam.reshape(C), dbet.reshape(C)


def solution(mesh):
    return jax.shard_map(
        shards,
        mesh=mesh,
        in_specs=(
            P("dp", "tm", "space", None, None),
            P("dp", None, None),
            P(),
            P(),
            P(("dp", "tm", "space"), None, None),
            P("dp", "tm", "space", None, None),
        ),
        out_specs=(
            P("dp", "tm", "space", None, None),
            P(("dp", "tm", "space"), None, None),
            P(),
            P(),
        ),
        check_vma=False,
    )
```

```python
import math

import jax
import jax.numpy as jnp
from jax import lax
from jax.experimental import pallas as pl
from jax.experimental.pallas import tpu as pltpu
from jax.sharding import PartitionSpec as P

MESH = pl.DeviceIdType.MESH
F32 = jnp.float32
BF16 = jnp.bfloat16
EPS = 1e-06

NDP, NTM, NSP = 8, 8, 4
GROUPS = 32
GS = 16
FR = 16
TILES = 4
CAP = 2
TH, TW = 8, 16
CELLS = TH * TW
C, COUT = 512, 256
TAPS = 27
ROWS = 9 * GS
LEFT = 48

B_TM, B_SP, A_SP, A_TM = 0, 8, 40, 44
L_SP, L_TM, WGT = 76, 80, 88
D_TM, D_DP, G_DP, D_SP, D_OWN, G_ALL = 112, 120, 136, 144, 176, 178
N_SEM = 210
HALVES = ((0, 14), (14, TAPS - 14))


def body(
    owner_ref, gamma_ref, beta_ref, lat_ref, ups_ref, w_ref,
    slab_ref, dw_ref, dgam_ref, dbet_ref,
    gz, ybuf, zsend, xbuf, wbuf, wf, wall, a9, xh, ds, dhb, rsd, dk, dsend, drecv, dsum,
    dxs, zback, ysend, gown, gdp, gsum, gall, send_sem, recv_sem, own_sem,
):
    d, z, y = lax.axis_index("dp"), lax.axis_index("tm"), lax.axis_index("space")
    ahead = lambda v, r, n: lax.rem(v + r, n)
    behind = lambda v, r, n: lax.rem(v - r + n, n)
    line = (d * NTM + z) * NSP + y
    place = lambda v: 4 * lax.rem(v, 2) + v // 2
    tz = place(z)
    mine = y * NTM + tz
    w_group = line // 8
    w_tm, w_sp = 2 * lax.rem(w_group, 4) + lax.rem(w_group, NTM) // 4, w_group // NTM
    w_piece = lax.rem(line, 8)
    src = lambda i: {
        "dp": mine // 4,
        "tm": 2 * lax.rem(mine, 4) + i // 4,
        "space": lax.rem(jnp.int32(i), 4) if not isinstance(i, int) else i % 4,
    }
    w_self = (w_tm == z) & (w_sp == y)
    w_home = d == mine // 4

    started = []

    def copy(a, b, n, to, m=None):
        return pltpu.make_async_remote_copy(
            src_ref=a, dst_ref=b, send_sem=send_sem.at[n], recv_sem=recv_sem.at[n if m is None else m],
            device_id=to, device_id_type=MESH,
        )

    def go(a, b, n, to, m=None):
        c = copy(a, b, n, to, m)
        c.start()
        started.append(c)
        return c

    def got(region, n):
        copy(region, region, n, {"tm": z}).wait_recv()

    barrier = pltpu.get_barrier_semaphore()

    def greet(to):
        pl.semaphore_signal(barrier, inc=1, device_id=to, device_id_type=MESH)

    pair = z + 1 - 2 * lax.rem(z, 2)
    for r in range(1, NSP):
        greet({"space": ahead(y, r, NSP)})
        greet({"tm": pair, "space": ahead(y, r, NSP)})
    greet({"tm": ahead(z, 1, NTM)})
    greet({"tm": behind(z, 1, NTM)})
    for r in range(1, NDP):
        greet({"dp": ahead(d, r, NDP)})

    p = lax.broadcasted_iota(jnp.int32, (CELLS, 4 * CELLS), 0)
    q = lax.broadcasted_iota(jnp.int32, (CELLS, 4 * CELLS), 1)
    pool = ((q >> 6) == (p >> 4)) & (((q & 31) >> 1) == (p & 15))
    pool = jnp.where(pool, 1.0, 0.0).astype(BF16)
    for f in range(2):
        pooled = jnp.dot(pool, ups_ref[f], preferred_element_type=F32)
        gz[2 * z + f, y] = pooled.astype(BF16)
    dhb[...] = jnp.zeros_like(dhb)
    dk[...] = jnp.zeros_like(dk)

    own_to = 8 * mine + d
    self_t = jnp.where(own_to == line, 1, 0)
    pl.semaphore_wait(barrier, 2 * (NSP - 1) + 2 + NDP - 1)

    def part_b(zo, yo, f=0, n=2):
        return gz.at[pl.ds(2 * zo + f, n), yo, pl.ds(LEFT, CELLS - LEFT)]

    def part_a(zo, yo, f=0, n=2):
        return gz.at[pl.ds(2 * zo + f, n), yo, pl.ds(0, LEFT)]

    zr, zl = {"tm": ahead(z, 1, NTM)}, {"tm": behind(z, 1, NTM)}
    yr, yl = {"space": ahead(y, 1, NSP)}, {"space": behind(y, 1, NSP)}
    yo_r, yo_l, yo_2 = ahead(y, 1, NSP), behind(y, 1, NSP), ahead(y, 2, NSP)

    def tm_step(region, base, h):
        frames = (dict(f=0, n=2),) * 2 if h < 4 else (dict(f=0, n=1), dict(f=1, n=1))
        for way, (to, o) in enumerate(((zr, behind(z, h - 1, NTM)), (zl, ahead(z, h - 1, NTM)))):
            a = region(o, **frames[way])
            go(a, a, base + 2 * (h - 1) + way, to)

    def tm_got(region, base, h):
        frames = (dict(f=0, n=2),) * 2 if h < 4 else (dict(f=0, n=1), dict(f=1, n=1))
        for way, o in enumerate((behind(z, h, NTM), ahead(z, h, NTM))):
            got(region(o, **frames[way]), base + 2 * (h - 1) + way)

    def sp_send(region, base, zo):
        a = region(zo, y)
        go(a, a, base, yr)
        go(a, a, base + 1, yl)

    def sp_forward(region, base, zo):
        got(region(zo, yo_l), base)
        a = region(zo, yo_l, 0, 1)
        go(a, a, base + 2, yr)
        got(region(zo, yo_r), base + 1)
        a = region(zo, yo_r, 1, 1)
        go(a, a, base + 3, yl)

    def sp_got(region, base, zo):
        got(region(zo, yo_2, 0, 1), base + 2)
        got(region(zo, yo_2, 1, 1), base + 3)

    steps = (0, -1, 1, -2, 2, -3, 3, 4)
    origin = [lax.rem(z + s + NTM, NTM) for s in steps]
    b_row = lambda zo, yo, f=0, n=2: part_b(zo, yo, f, n)
    b_tm = lambda zo, f=0, n=2: part_b(zo, y, f, n)

    sides = (y, yo_l, yo_r, yo_2)
    a_tm = [lambda zo, f=0, n=2, yo=yo: part_a(zo, yo, f, n) for yo in sides]
    near = [(0,), (1, 2), (3, 4), (5, 6), (7,)]

    def wave_b(h):
        tm_got(b_tm, B_TM, h)
        if h < 4:
            tm_step(b_tm, B_TM, h + 1)
        for b in near[h]:
            sp_send(b_row, B_SP + 4 * b, origin[b])

    def wave_a(h):
        for q in range(4):
            tm_got(a_tm[q], A_TM + 8 * q, h)
            if h < 4:
                tm_step(a_tm[q], A_TM + 8 * q, h + 1)

    def forward(h):
        for b in near[h]:
            sp_forward(b_row, B_SP + 4 * b, origin[b])

    def complete(h):
        for b in near[h]:
            sp_got(b_row, B_SP + 4 * b, origin[b])

    def block(h, i):
        return lax.rem(z + (2 * i - 1) * h + NTM, NTM)

    cell = lax.broadcasted_iota(jnp.int32, (8, GS, CELLS), 2)
    ix, iy = cell & (TW - 1), cell >> 4

    def inside(dy, dx):
        ok = None
        for cond in (
            [iy + dy >= 0] if dy < 0 else [iy + dy < TH] if dy > 0 else []
        ) + ([ix + dx >= 0] if dx < 0 else [ix + dx < TW] if dx > 0 else []):
            ok = cond if ok is None else ok & cond
        return ok

    nt = (((1,), (1,)), ((), ()))

    def dhidden(h):
        def frame(n, _):
            f = 2 * block(h, n // 2) + lax.rem(n, 2)
            v = lax.dot_general(
                wall[...], gz[f].reshape(TILES * CELLS, COUT), nt, preferred_element_type=F32
            )
            for t in range(TILES):
                lanes = slice(t * CELLS, (t + 1) * CELLS)
                rsd[TILES * f + t] = v[3 * ROWS :, lanes]
                for kt in range(3):
                    out = None
                    for s in range(9):
                        dy, dx = s // 3 - 1, s % 3 - 1
                        w = v[kt * ROWS + s * GS : kt * ROWS + (s + 1) * GS, lanes]
                        if s != 4:
                            w = pltpu.roll(w, (TW * dy + dx) % CELLS, 1)
                            w = jnp.where(inside(-dy, -dx)[0], w, 0.0)
                        out = w if out is None else out + w
                    dhb[TILES * (f + kt) + t] += out
            return 0

        lax.fori_loop(0, 2 * len(near[h]), frame, 0)

    def dweight(h):
        def one(n, _):
            i = block(h, n)
            g = gz[pl.ds(2 * i, 2)].reshape(1024, COUT)
            for kt in range(3):
                a = a9[:, pl.ds(pl.multiple_of(1024 * i + 512 * kt, 512), 1024)]
                dk[9 * kt : 9 * kt + 9] += jnp.dot(a, g, preferred_element_type=F32).reshape(9, GS, COUT)
            return 0

        lax.fori_loop(0, len(near[h]), one, 0)

    sp_send(part_a, A_SP, z)
    tm_step(b_tm, B_TM, 1)
    sp_send(b_row, B_SP, z)

    to_group = copy(w_ref, wbuf.at[w_piece], WGT + 8, {"tm": w_tm, "space": w_sp}, WGT + w_piece)

    @pl.when(jnp.logical_not(w_self))
    def _():
        to_group.start()

    @pl.when(w_self)
    def _():
        pltpu.make_async_copy(w_ref, wbuf.at[w_piece], recv_sem.at[WGT + w_piece]).start()

    wave_b(1)
    sp_forward(part_a, A_SP, z)
    for q in range(3):
        tm_step(a_tm[q], A_TM + 8 * q, 1)
    wave_b(2)

    for r in range(1, NSP):
        yo = ahead(y, r, NSP)
        go(
            lat_ref.at[:, :, :, pl.ds(pl.multiple_of(yo * 128, 128), 128)],
            ybuf.at[y], L_SP + r, {"space": yo},
        )
    own = pltpu.make_async_copy(
        lat_ref.at[:, :, :, pl.ds(pl.multiple_of(y * 128, 128), 128)], ybuf.at[y], own_sem.at[0]
    )
    own.start()

    sp_got(part_a, A_SP, z)
    tm_step(a_tm[3], A_TM + 24, 1)
    forward(0)

    @pl.when(w_home)
    def _():
        for i in range(8):
            got(wbuf.at[i], WGT + i)
        for r in range(1, NDP):
            copy(wbuf, wbuf, WGT + 9 + r, {"dp": ahead(d, r, NDP)}, WGT + 9).start()

    wave_b(3)
    wave_a(1)
    wave_b(4)

    own.wait()
    for r in range(1, NSP):
        got(ybuf.at[behind(y, r, NSP)], L_SP + r)
    owners = [owner_ref[t] for t in range(TILES)]
    ranks = [
        jnp.minimum(
            sum([(owners[u] == owners[t]).astype(jnp.int32) for u in range(t)], jnp.int32(0)), CAP - 1
        )
        for t in range(TILES)
    ]
    for t in range(TILES):
        for f in range(2):
            v = ybuf[owners[t], f, ranks[t]].astype(F32)
            zsend[:, f * TILES + t] = v.T.reshape(NTM, GS, CELLS).astype(BF16)
    for r in range(1, NTM):
        zo = ahead(z, r, NTM)
        go(zsend.at[place(zo)], xbuf.at[z], L_TM + r, {"tm": zo})
    xbuf[z] = zsend[tz]

    @pl.when(jnp.logical_not(w_home))
    def _():
        got(wbuf, WGT + 9)

    for i in range(8):
        wf[:, 2 * i : 2 * i + 2, :] = wbuf[i].astype(F32)
    wall[0 : 3 * ROWS, :] = wf[...].reshape(3 * ROWS, COUT).astype(BF16)
    pick_r = lax.broadcasted_iota(jnp.int32, (GS, COUT), 0)
    pick_o = lax.broadcasted_iota(jnp.int32, (GS, COUT), 1)
    wall[3 * ROWS : 3 * ROWS + GS, :] = jnp.where(pick_o == mine * GS + pick_r, 1.0, 0.0).astype(BF16)

    forward(1)
    complete(0)
    dhidden(0)
    wave_a(2)
    forward(2)
    complete(1)
    dhidden(1)

    for r in range(1, NTM):
        got(xbuf.at[behind(z, r, NTM)], L_TM + r)
    count = float(FR * TILES * CELLS * GS)
    zero = jnp.zeros((GS, CELLS), F32)

    def whole(v):
        return jnp.sum(jnp.sum(v, axis=1, keepdims=True), axis=0, keepdims=True)

    def total(i, acc):
        return acc + jnp.sum(xbuf[i].astype(F32), axis=0)

    mean = whole(lax.fori_loop(0, NTM, total, zero)) / count

    def spread(i, acc):
        v = xbuf[i].astype(F32) - mean
        return acc + jnp.sum(v * v, axis=0)

    inverse = lax.rsqrt(whole(lax.fori_loop(0, NTM, spread, zero)) / count + EPS)

    row16 = lax.broadcasted_iota(jnp.int32, (GS, CELLS), 0)
    lane16 = lax.broadcasted_iota(jnp.int32, (GS, CELLS), 1)
    diag = lane16 == tz * GS + row16

    def column(ref):
        return jnp.sum(jnp.where(diag, ref[pl.ds(y, 1), :], 0.0), axis=1, keepdims=True)

    gamma, beta = column(gamma_ref), column(beta_ref)

    def taps(i, _):
        normed = (xbuf[i].astype(F32) - mean) * inverse
        act = normed * gamma + beta
        sig = jax.nn.sigmoid(act)
        xh[i] = normed
        ds[i] = sig * (1.0 + act * (1.0 - sig))
        hidden = (act * sig).astype(BF16).astype(F32)
        base = pl.multiple_of((i + 1) * 1024, 1024)
        for s in range(9):
            dy, dx = s // 3 - 1, s % 3 - 1
            v = hidden
            if s != 4:
                v = pltpu.roll(v, (-(TW * dy + dx)) % CELLS, 2)
                v = jnp.where(inside(dy, dx), v, 0.0)
            v = v.astype(BF16)
            for j in range(8):
                a9[s * GS : (s + 1) * GS, pl.ds(base + j * CELLS, CELLS)] = v[j]
        return 0

    lax.fori_loop(0, NTM, taps, 0)
    a9[:, 0:512] = a9[:, 1024:1536]
    a9[:, 512:1024] = a9[:, 1024:1536]

    wave_a(3)
    forward(3)
    dweight(0)
    dweight(1)
    complete(2)
    dhidden(2)
    dweight(2)
    forward(4)
    complete(3)
    dhidden(3)
    dweight(3)
    wave_a(4)
    complete(4)
    dweight(4)

    dhidden(4)
    dhb[8:12] = dhb[8:12] + (dhb[0:4] + dhb[4:8])

    def gains(i, acc):
        dact = dhb[pl.ds(8 + 8 * i, 8)] * ds[i]
        dhb[pl.ds(8 + 8 * i, 8)] = dact
        return acc[0] + jnp.sum(dact * xh[i], axis=0), acc[1] + jnp.sum(dact, axis=0)

    dgam, dbet = lax.fori_loop(0, NTM, gains, (zero, zero))
    dgam = jnp.sum(dgam, axis=1, keepdims=True)
    dbet = jnp.sum(dbet, axis=1, keepdims=True)
    m1 = jnp.sum(dbet * gamma, axis=0, keepdims=True) / count
    m2 = jnp.sum(dgam * gamma, axis=0, keepdims=True) / count

    def dinput(i, _):
        v = inverse * (dhb[pl.ds(8 + 8 * i, 8)] * gamma - m1 - xh[i] * m2)
        dxs[i] = (v + rsd[pl.ds(8 * i, 8)]).astype(BF16)
        return 0

    lax.fori_loop(0, NTM, dinput, 0)

    for r in range(1, NTM):
        zo = ahead(z, r, NTM)
        go(dxs.at[zo], zback.at[tz], D_TM + r, {"tm": zo})
    zback[tz] = dxs[z]

    rscale = 1.0 / math.sqrt(NDP * FR * TILES * CELLS)
    for i in range(8):
        dsend[i] = dk[:, 2 * i : 2 * i + 2, :] * rscale
    for h, (k0, kn) in enumerate(HALVES):
        for r in range(1, NDP):
            to = ahead(d, r, NDP)
            go(
                dsend.at[to, pl.ds(k0, kn)], drecv.at[d, pl.ds(k0, kn)], D_DP + 8 * h + r, {"dp": to}
            )
    drecv[d] = dsend[d]

    gown[0:1, :] = jnp.sum(jnp.where(diag, dgam * rscale, 0.0), axis=0, keepdims=True)
    gown[1:2, :] = jnp.sum(jnp.where(diag, dbet * rscale, 0.0), axis=0, keepdims=True)
    for r in range(1, NDP):
        to = ahead(d, r, NDP)
        go(gown, gdp.at[d], G_DP + r, {"dp": to})
    gdp[d] = gown[...]

    held = []
    for yo in range(NSP):
        for j in range(CAP):
            held.append([(owners[t] == yo) & (ranks[t] == j) for t in range(TILES)])
    nearest = (0, 1, 7, 2, 6, 3, 5, 4)

    def to_slots(k):
        r = nearest[k]
        p = place(behind(z, r, NTM))
        if r:
            got(zback.at[p], D_TM + r)
        tiles = [zback[p, i] for i in range(2 * TILES)]
        for yo in range(NSP):
            for j in range(CAP):
                for f in range(2):
                    v = jnp.zeros((GS, CELLS), BF16)
                    for t in range(TILES):
                        v = jnp.where(held[CAP * yo + j][t], tiles[f * TILES + t], v)
                    ysend[p, yo, f, j] = v
        for r in range(1, NSP):
            yo = ahead(y, r, NSP)
            go(ysend.at[p, yo], slab_ref.at[y, p], D_SP + 4 * k + r, {"space": yo})

    for k in range(3):
        to_slots(k)

    for r in range(1, NDP):
        got(gdp.at[behind(d, r, NDP)], G_DP + r)
    acc = gdp[0]
    for i in range(1, NDP):
        acc = acc + gdp[i]
    gsum[...] = acc
    for r in range(NTM):
        for q in range(NSP):
            if r or q:
                to = {"tm": ahead(z, r, NTM), "space": ahead(y, q, NSP)}
                go(gsum, gall.at[z, y], G_ALL + r * NSP + q, to)
    gall[z, y] = gsum[...]

    for k in range(3, NTM):
        to_slots(k)
    own = pltpu.make_async_copy(ysend.at[:, y], slab_ref.at[y], own_sem.at[1])
    own.start()

    for h, (k0, kn) in enumerate(HALVES):
        half = pl.ds(k0, kn)
        for r in range(1, NDP):
            got(drecv.at[behind(d, r, NDP), half], D_DP + 8 * h + r)
        acc = drecv[0, k0 : k0 + kn]
        for i in range(1, NDP):
            acc = acc + drecv[i, k0 : k0 + kn]
        dsum[k0 : k0 + kn] = acc
        to_owner = copy(dsum.at[half], dw_ref.at[half], D_OWN + h, src(d))

        @pl.when(self_t == 0)
        def _():
            to_owner.start()

        @pl.when(self_t == 1)
        def _():
            pltpu.make_async_copy(dsum.at[half], dw_ref.at[half], recv_sem.at[D_OWN + h]).start()

    for r in range(NTM):
        for q in range(NSP):
            if r or q:
                got(gall.at[behind(z, r, NTM), behind(y, q, NSP)], G_ALL + r * NSP + q)
    for s in range(NSP):
        acc = gall[0, s]
        for i in range(1, NTM):
            acc = acc + gall[i, s]
        dgam_ref[s : s + 1, :] = acc[0:1]
        dbet_ref[s : s + 1, :] = acc[1:2]

    own.wait()
    for k in range(NTM):
        p = place(behind(z, nearest[k], NTM))
        for r in range(1, NSP):
            got(slab_ref.at[behind(y, r, NSP), p], D_SP + 4 * k + r)
    for h, (k0, kn) in enumerate(HALVES):
        got(dw_ref.at[pl.ds(k0, kn)], D_OWN + h)
    for c in started:
        c.wait_send()

    @pl.when(self_t == 0)
    def _():
        for h, (k0, kn) in enumerate(HALVES):
            half = pl.ds(k0, kn)
            copy(dsum.at[half], dw_ref.at[half], D_OWN + h, src(d)).wait_send()

    @pl.when(jnp.logical_not(w_self))
    def _():
        copy(w_ref, wbuf.at[w_piece], WGT + 8, {"tm": z}).wait_send()

    @pl.when(w_home)
    def _():
        for r in range(1, NDP):
            copy(wbuf, wbuf, WGT + 9 + r, {"dp": ahead(d, r, NDP)}, WGT + 9).wait_send()


def written(slab_ref, *refs):
    for f in range(2):
        for j in range(CAP):
            for q in range(NSP):
                v = slab_ref[q, :, f, j].astype(F32).reshape(128, CELLS)
                refs[3][f, j, :, 128 * q : 128 * (q + 1)] = v.T.astype(BF16)
    for a, b in zip(refs[:3], refs[4:]):
        b[...] = a[...]


def shards(latents, owner, gamma, beta, weight, upstream):
    vmem = pl.BlockSpec(memory_space=pltpu.VMEM)
    hbm = pl.BlockSpec(memory_space=pl.ANY)
    scratch = [
        ((FR, TILES, CELLS, COUT), BF16),
        ((NSP, 2, CAP, CELLS, 128), BF16),
        ((NTM, 8, GS, CELLS), BF16),
        ((NTM, 8, GS, CELLS), BF16),
        ((8, TAPS, 2, COUT), BF16),
        ((TAPS, GS, COUT), F32),
        ((3 * ROWS + GS, COUT), BF16),
        ((ROWS, 512 * (FR + 2)), BF16),
        ((NTM, 8, GS, CELLS), F32),
        ((NTM, 8, GS, CELLS), F32),
        ((TILES * (FR + 2), GS, CELLS), F32),
        ((TILES * FR, GS, CELLS), F32),
        ((TAPS, GS, COUT), F32),
        ((8, TAPS, 2, COUT), F32),
        ((8, TAPS, 2, COUT), F32),
        ((TAPS, 2, COUT), F32),
        ((NTM, 8, GS, CELLS), BF16),
        ((NTM, 8, GS, CELLS), BF16),
        ((NTM, NSP, 2, CAP, GS, CELLS), BF16),
        ((2, 128), F32),
        ((NDP, 2, 128), F32),
        ((2, 128), F32),
        ((NTM, NSP, 2, 128), F32),
    ]
    slab, dw, dgam, dbet = pl.pallas_call(
        body,
        out_shape=(
            jax.ShapeDtypeStruct((NSP, NTM, 2, CAP, GS, CELLS), BF16),
            jax.ShapeDtypeStruct((TAPS, 2, COUT), F32),
            jax.ShapeDtypeStruct((4, 128), F32),
            jax.ShapeDtypeStruct((4, 128), F32),
        ),
        in_specs=[pl.BlockSpec(memory_space=pltpu.SMEM), vmem, vmem, vmem, vmem, vmem],
        out_specs=(hbm, hbm, vmem, vmem),
        scratch_shapes=[pltpu.VMEM(s, t) for s, t in scratch]
        + [
            pltpu.SemaphoreType.DMA((N_SEM,)),
            pltpu.SemaphoreType.DMA((N_SEM,)),
            pltpu.SemaphoreType.DMA((3,)),
        ],
        compiler_params=pltpu.CompilerParams(
            collective_id=0, has_side_effects=True, vmem_limit_bytes=56 * 2**20
        ),
    )(
        owner.reshape(TILES),
        gamma.reshape(4, 128),
        beta.reshape(4, 128),
        latents[0],
        upstream.reshape(2, 4 * CELLS, COUT),
        weight.transpose(1, 0, 2),
    )
    dlat, dw, dgam, dbet = pl.pallas_call(
        written,
        out_shape=[jax.ShapeDtypeStruct((2, CAP, CELLS, C), BF16)]
        + [jax.ShapeDtypeStruct(v.shape, v.dtype) for v in (dw, dgam, dbet)],
        in_specs=[vmem] * 4,
        out_specs=[vmem] * 4,
    )(slab, dw, dgam, dbet)
    return dlat[None], dw.transpose(1, 0, 2), dgam.reshape(C), dbet.reshape(C)


def solution(mesh):
    return jax.shard_map(
        shards,
        mesh=mesh,
        in_specs=(
            P("dp", "tm", "space", None, None),
            P("dp", None, None),
            P(),
            P(),
            P(("dp", "tm", "space"), None, None),
            P("dp", "tm", "space", None, None),
        ),
        out_specs=(
            P("dp", "tm", "space", None, None),
            P(("dp", "tm", "space"), None, None),
            P(),
            P(),
        ),
        check_vma=False,
    )
```
